32 devices in a mesh: group: 4 (over x, core), dev: 8 (over z, y).
Axes of the slice: x: 2, y: 2, z: 4, core: 2. Of those that a mesh axis runs over, the one named last changes fastest.
Arguments:
- queries: bfloat16 [256, 32, 128], P(('group', 'dev')), may hold values from -0.5390625 to 0.5390625
- passages: bfloat16 [512, 256, 128], P(('group', 'dev')), may hold values from -6 to 6
- candidates: int32 [256, 16], P(('group', 'dev')), may hold values from 0 to 511, as said below
- location: int32 [512], replicated, may hold values from 0 to 511, as said below
Outputs:
- loss: float32 [256], P(('group', 'dev'))
- query_grad: float32 [256, 32, 128], P(('group', 'dev'))
The draws below stay inside these ranges and needn't reach their ends.
Inputs may be any that keep to these rules, and one draw needn't show every extreme that they name: `candidates`: for each device holding queries and each device holding passage rows (rows of passages split evenly over group+dev in order), at most 12 of the sending device's pairs (query, listed document) have their document's row on that device. In every draw one device receives exactly 12 such pairs from every device. `location`: A permutation of the documents.
All inputs are finite; a program needn't handle non-finite values.
Results may differ from the reference program's by a relative error of at most 0.011.
Values may be sent and summed in bfloat16 or wider, within the bound.
No kernel may reach another device: no remote copies, remote signals or barrier semaphores. Data moves between devices by JAX's collectives and lax.ppermute only.
A program may use at most 64 MiB of HBM per device.

```python
import jax
import jax.numpy as jnp
from jax import lax

E = 128
QT = 32
PT = 256
CAND = 16
QD = 8
PD = 16
CAP = 12
QUERIES = 256
NPASS = 512
DEVICES = 32


def layout(key):
    base = jax.random.fold_in(key, 7)
    key_perm, key_hot, key_order, key_local = jax.random.split(base, 4)
    location = jax.random.permutation(key_perm, NPASS).astype(jnp.int32)
    hot_target = jax.random.randint(key_hot, (), 0, DEVICES)
    slot_total = DEVICES * CAP
    pair_count = QD * CAND

    def choose_slots(one_key):
        key_first, key_second = jax.random.split(one_key)
        ranking = jax.random.permutation(key_first, slot_total).astype(jnp.int32)
        owners = jnp.arange(slot_total, dtype=jnp.int32) // CAP
        ranking = jnp.where(owners == hot_target, ranking - slot_total, ranking)
        chosen = jnp.argsort(ranking)[:pair_count].astype(jnp.int32)
        return jax.random.permutation(key_second, chosen)
    chosen = jax.vmap(choose_slots)(jax.random.split(key_order, DEVICES))
    target = chosen // CAP
    local_row = jax.random.randint(key_local, (DEVICES, pair_count), 0, PD)
    rows = (target * PD + local_row).reshape(QUERIES, CAND)
    inverse = jnp.argsort(location).astype(jnp.int32)
    return (inverse[rows].astype(jnp.int32), location)


def draw_candidates(key, part):
    return layout(key)[0]


def draw_location(key, part):
    return layout(key)[1]


def block_scale(own_key, extent, shards, low, top_value):
    gain, own = 1.0, jax.random.fold_in(own_key, 6)
    for position, shards_of in shards:
        draws = jnp.exp(jax.random.uniform(jax.random.fold_in(own, position), (shards_of,), jnp.float32, low / len(shards), top_value / len(shards)))
        gain = gain * jnp.repeat(draws, extent[position] // shards_of).reshape([-1 if axis == position else 1 for axis in range(len(extent))])
    return gain


def centred(stream_key, shape, scale, reach, cuts=(), kind=jnp.bfloat16):
    array = scale * jax.random.normal(stream_key, shape, jnp.float32)
    if cuts:
        array = array * block_scale(stream_key, shape, cuts, -0.22, 0.18)
    return jnp.clip(array, -reach, reach).astype(kind)


def setup_inputs(seed: int = 0) -> dict:
    key_list = jax.random.split(jax.random.key(seed), 5)
    queries = centred(key_list[0], (QUERIES, QT, E), 0.09, 0.5390625, ((0, 32),))
    passages = centred(key_list[1], (NPASS, PT, E), 1.0, 6.0, ((0, 32),))
    candidates = draw_candidates(jax.random.fold_in(key_list[4], 71), 0)
    location = draw_location(jax.random.fold_in(key_list[4], 71), 0)
    return {"queries": queries, "passages": passages, "candidates": candidates, "location": location}


SOFTNESS = 0.02
EPSILON = 1e-06

def normalize(values):
    floats = values.astype(jnp.float32)
    scale = lax.rsqrt(lax.optimization_barrier(jnp.sum(floats * floats, axis=-1, keepdims=True)) + EPSILON)
    return (floats * scale, scale)

def reference(queries, passages, candidates, location):
    query_unit, query_scale = normalize(queries)
    query_send = query_unit.astype(jnp.bfloat16)
    passage_unit = normalize(passages)[0].astype(jnp.bfloat16)
    rows = location[candidates].astype(jnp.int32)

    def one_block(inputs):
        query_block, row_block = inputs
        passage_block = passage_unit[row_block].astype(jnp.float32)
        logits = jnp.einsum('bqe,bkpe->bkqp', query_block.astype(jnp.float32), passage_block) / SOFTNESS
        exp_terms = jnp.exp(logits)
        token_mass = lax.optimization_barrier(jnp.sum(exp_terms, axis=-1, keepdims=True))
        pair_score = lax.optimization_barrier(jnp.sum(SOFTNESS * jnp.log(token_mass[..., 0]), axis=-1))
        attention = (exp_terms / token_mass).astype(jnp.bfloat16)
        pulled = jnp.einsum('bkqp,bkpe->bkqe', attention.astype(jnp.float32), passage_block).astype(jnp.bfloat16)
        return (pulled, pair_score)
    blocks = QUERIES // QD
    pulled, pair_score = lax.map(one_block, (query_send.reshape(blocks, QD, QT, E), rows.reshape(blocks, QD, CAND)))
    pulled = pulled.reshape(QUERIES, CAND, QT, E)
    pair_score = pair_score.reshape(QUERIES, CAND)
    exp_scores = jnp.exp(pair_score)
    total = lax.optimization_barrier(jnp.sum(exp_scores, axis=-1, keepdims=True))
    loss = jnp.log(total[:, 0]) - pair_score[:, 0]
    first = (jnp.arange(CAND) == 0).astype(jnp.float32)
    coeff = exp_scores / total - first[None, :]
    unit_grad = jnp.einsum('bk,bkqe->bqe', coeff, pulled.astype(jnp.float32))
    along = lax.optimization_barrier(jnp.sum(query_unit * unit_grad, axis=-1, keepdims=True))
    query_grad = (unit_grad - query_unit * along) * query_scale
    return (loss, query_grad)
```

```python
import functools

import jax
import jax.numpy as jnp
from jax import lax
from jax.experimental import pallas as pl
from jax.experimental.pallas import tpu as pltpu
from jax.sharding import PartitionSpec as P

SOFTNESS = 0.02
EPSILON = 1e-06
LANES = 128
TAIL = 16
BASE = 256
UNROLL = 4
F32 = jnp.float32
BF16 = jnp.bfloat16


def call(body, out_shape, name, flops=0, in_specs=None, scratch=()):
    kwargs = {} if in_specs is None else {"in_specs": in_specs}
    return pl.pallas_call(
        body,
        out_shape=out_shape,
        scratch_shapes=list(scratch),
        name=name,
        cost_estimate=pl.CostEstimate(flops=flops, bytes_accessed=1 << 20, transcendentals=0),
        compiler_params=pltpu.CompilerParams(vmem_limit_bytes=48 * 1024 * 1024),
        **kwargs,
    )


def unit(values):
    floats = values.astype(F32)
    scale = lax.rsqrt(jnp.sum(floats * floats, axis=-1, keepdims=True) + EPSILON)
    return floats * scale, scale


def pack_body(queries_ref, cand_ref, out_ref):
    count, length, width = queries_ref.shape
    rows = count * length
    out_ref[:rows] = unit(queries_ref[...])[0].astype(BF16).reshape(rows, width)
    ids = jnp.broadcast_to(cand_ref[...], (TAIL, LANES))
    high = ids // BASE
    low = ids - high * BASE
    place = lax.broadcasted_iota(jnp.int32, (TAIL, LANES), 0)
    digits = jnp.where(place == 0, high, jnp.where(place == 1, low, 0))
    out_ref[rows:] = digits.astype(F32).astype(BF16)


def unit_body(passages_ref, out_ref):
    def step(index, carry):
        out_ref[index] = unit(passages_ref[index])[0].astype(BF16)
        return carry

    lax.fori_loop(0, passages_ref.shape[0], step, 0)


def route_body(docs_ref, pay_ref, out_ref, *, rows, near_count, slots):
    blocks = pay_ref.shape[0]
    ids = []
    for block in range(blocks):
        tile = pay_ref[block, rows : rows + TAIL].astype(F32)
        ids.append((tile[0:1] * BASE + tile[1:2]).astype(jnp.int32))
    ids = jnp.concatenate(ids, axis=0)
    pair = lax.broadcasted_iota(jnp.int32, (blocks, LANES), 0) * LANES
    pair = pair + lax.broadcasted_iota(jnp.int32, (blocks, LANES), 1)
    upper = lax.broadcasted_iota(jnp.int32, (LANES, LANES), 0)
    lane = lax.broadcasted_iota(jnp.int32, (LANES, LANES), 1)
    triangle = (upper <= lane).astype(F32)
    diagonal = upper == lane
    place = lax.broadcasted_iota(jnp.int32, (slots, LANES), 0).astype(F32)
    for half in range(2):
        local = jnp.full((blocks, LANES), -1, jnp.int32)
        for index in range(near_count):
            local = jnp.where(ids == docs_ref[half * near_count + index], index, local)
        mask = local >= 0
        code = (local * (blocks * LANES) + pair).astype(F32)
        ranks = jnp.dot(mask.astype(F32), triangle, preferred_element_type=F32)
        before = jnp.zeros((1, 1), F32)
        found = jnp.zeros((slots, LANES), F32)
        for block in range(blocks):
            row = ranks[block : block + 1]
            slot = jnp.where(mask[block : block + 1], before + row - 1.0, -1.0)
            found = found + jnp.where(place == slot, code[block : block + 1], 0.0)
            before = before + row[:, LANES - 1 : LANES]
        packed = jnp.sum(found, axis=1, keepdims=True)
        for part in range(slots // LANES):
            piece = packed[part * LANES : (part + 1) * LANES]
            line = jnp.sum(jnp.where(diagonal, piece, 0.0), axis=0, keepdims=True)
            out_ref[half, part : part + 1] = line.astype(jnp.int32)
        out_ref[half, slots // LANES : slots // LANES + 1] = jnp.broadcast_to(
            before, (1, LANES)
        ).astype(jnp.int32)


def score_pairs(list_ref, pay_ref, pass_ref, acc_ref, sums_ref, *, length, list_len):
    parts = list_ref.shape[0] - 1
    blocks = pay_ref.shape[0]
    per_block = LANES // list_len
    queries = blocks * per_block
    count = list_ref[parts, 0]
    ones = jnp.ones((pass_ref.shape[1], LANES), BF16)

    def step(index, carry):
        done = []
        for offset in range(UNROLL):
            slot = index * UNROLL + offset
            code = list_ref[slot // LANES, slot % LANES]
            local = code // (blocks * LANES)
            pair = code % (blocks * LANES)
            query = pair // list_len
            first = (pair % list_len) == 0
            weight = jnp.where(slot < count, 1.0, 0.0).astype(F32)
            row = pl.multiple_of((query % per_block) * length, length)
            tokens = pay_ref[query // per_block, pl.ds(row, length)]
            passage = pass_ref[local]
            logits = lax.dot_general(
                tokens, passage, (((1,), (1,)), ((), ())), preferred_element_type=F32
            )
            terms = jnp.exp(logits * (1.0 / SOFTNESS)).astype(BF16)
            pulled = jnp.dot(terms, passage, preferred_element_type=F32)
            mass = jnp.dot(terms, ones, preferred_element_type=F32)
            pulled = pulled / mass
            score = SOFTNESS * jnp.sum(jnp.log(mass), axis=0, keepdims=True)
            exp_score = jnp.exp(score)
            target = jnp.where(first, queries, 0) + query
            factor = jnp.where(first, 1.0, exp_score) * weight
            value = jnp.where(first, score, exp_score) * weight
            done.append((target, pulled * factor, value))
        for target, product, value in done:
            at = pl.ds(pl.multiple_of(target * length, length), length)
            acc_ref[at] = acc_ref[at] + product
            sums_ref[pl.ds(target, 1)] = sums_ref[pl.ds(target, 1)] + value
        return carry

    lax.fori_loop(0, (count + UNROLL - 1) // UNROLL, step, 0)


def near_body(list_ref, pay_ref, pass_ref, acc_ref, sums_ref, *, length, list_len):
    acc_ref[...] = jnp.zeros_like(acc_ref)
    sums_ref[...] = jnp.zeros_like(sums_ref)
    score_pairs(list_ref, pay_ref, pass_ref, acc_ref, sums_ref, length=length, list_len=list_len)


def far_body(
    list_ref, pay_ref, pass_ref, acc_in, sums_in, send_ref, keep_ref, sums_ref, acc_ref,
    *, length, list_len,
):
    acc_ref[...] = acc_in[...]
    sums_ref[...] = sums_in[...]
    score_pairs(list_ref, pay_ref, pass_ref, acc_ref, sums_ref, length=length, list_len=list_len)
    half = send_ref.shape[1]
    for kind in range(2):
        start = kind * 2 * half
        keep_ref[kind] = acc_ref[start : start + half]
        send_ref[kind] = acc_ref[start + half : start + 2 * half].astype(BF16)


def merge_body(keep_ref, got_ref, sums_ref, send_ref, rest_ref, *, length):
    queries = sums_ref.shape[1]

    def part(index):
        at = pl.ds(pl.multiple_of(index * length, length), length)
        others = keep_ref[0, at] + got_ref[0, at].astype(F32)
        first = keep_ref[1, at] + got_ref[1, at].astype(F32)
        return others - sums_ref[0, pl.ds(index, 1)] * first

    def step(index, carry):
        at = pl.ds(pl.multiple_of(index * length, length), length)
        rest_ref[at] = part(index)
        send_ref[at] = part(index + queries // 2).astype(BF16)
        return carry

    lax.fori_loop(0, queries // 2, step, 0)


def last_body(queries_ref, keep_ref, got_ref, sums_ref, grad_ref, loss_ref, *, length):
    for index in range(queries_ref.shape[0]):
        at = slice(index * length, (index + 1) * length)
        spread = sums_ref[0, index : index + 1]
        score = sums_ref[1, index : index + 1]
        total = spread + jnp.exp(score)
        loss_ref[index : index + 1] = jnp.log(total) - score
        gradient = (keep_ref[at] + got_ref[at].astype(F32)) / total
        query_unit, query_scale = unit(queries_ref[index])
        along = jnp.sum(query_unit * gradient, axis=-1, keepdims=True)
        grad_ref[index] = (gradient - query_unit * along) * query_scale


def swap(value, axis, bit):
    size = lax.axis_size(axis)
    return lax.ppermute(value, axis, [(index, index ^ bit) for index in range(size)])


def bits_of(size):
    return [1 << power for power in reversed(range(size.bit_length() - 1))]


def local(queries, passages, candidates, location):
    group_count = lax.axis_size("group")
    dev_count = lax.axis_size("dev")
    device_total = group_count * dev_count
    query_count, length, width = queries.shape
    pass_count, pass_len, _ = passages.shape
    list_len = candidates.shape[1]
    pair_count = query_count * list_len
    rows = query_count * length
    slot_cap = max(2, (3 * pair_count + device_total - 1) // device_total)
    group = lax.axis_index("group")
    dev = lax.axis_index("dev")
    shape = jax.ShapeDtypeStruct

    units = call(unit_body, shape(passages.shape, BF16), "passage_units")(passages)
    payload = call(pack_body, shape((rows + TAIL, width), BF16), "query_units")(
        queries, candidates.reshape(1, pair_count)
    )

    held, offsets = [units], [0]
    for bit in bits_of(group_count):
        held = held + [swap(block, "group", bit) for block in held]
        offsets = offsets + [offset ^ bit for offset in offsets]
    half_bit = group_count // 2
    order = [index for index, offset in enumerate(offsets) if not offset & half_bit]
    order += [index for index, offset in enumerate(offsets) if offset & half_bit]
    near_blocks = len(order) // 2
    near = jnp.concatenate([held[index] for index in order[:near_blocks]], axis=0)
    far = jnp.concatenate([held[index] for index in order[near_blocks:]], axis=0)

    owners = (group ^ jnp.array([offsets[index] for index in order], jnp.int32)) * dev_count + dev
    held_rows = owners[:, None] * pass_count + jnp.arange(pass_count, dtype=jnp.int32)[None, :]
    hits = location[None, :] == held_rows.reshape(-1, 1)
    documents = jnp.arange(location.shape[0], dtype=jnp.int32)
    docs = jnp.sum(jnp.where(hits, documents[None, :], 0), axis=1)

    pay = payload[None]
    for bit in bits_of(dev_count):
        pay = jnp.concatenate([pay, swap(pay, "dev", bit)], axis=0)

    near_count = near_blocks * pass_count
    most = dev_count * min(pair_count, near_blocks * slot_cap)
    slots = -(-most // LANES) * LANES
    lists = call(
        functools.partial(route_body, rows=rows, near_count=near_count, slots=slots),
        shape((2, slots // LANES + 1, LANES), jnp.int32),
        "route",
        in_specs=[pl.BlockSpec(memory_space=pltpu.SMEM), pl.BlockSpec(memory_space=pltpu.VMEM)],
    )(docs, pay)

    all_queries = dev_count * query_count
    flops = dev_count * pair_count // 4 * length * pass_len * width * 4
    mem = [pl.BlockSpec(memory_space=pltpu.SMEM)] + [pl.BlockSpec(memory_space=pltpu.VMEM)] * 4
    sizes = dict(length=length, list_len=list_len)
    acc, sums = call(
        functools.partial(near_body, **sizes),
        [shape((2 * all_queries * length, width), F32), shape((2 * all_queries, LANES), F32)],
        "score_near",
        flops,
        mem[:3],
    )(lists[0], pay, near)
    half_rows = all_queries * length // 2
    send, keep, sums = call(
        functools.partial(far_body, **sizes),
        [
            shape((2, half_rows, width), BF16),
            shape((2, half_rows, width), F32),
            shape((2 * all_queries, LANES), F32),
        ],
        "score_far",
        flops,
        mem,
        [pltpu.VMEM((2 * all_queries * length, width), F32)],
    )(lists[1], pay, far, acc, sums)

    steps = bits_of(dev_count)[::-1]
    sums = sums.reshape((2, 2, all_queries // 2, LANES))
    sums = sums[:, 0] + swap(sums[:, 1], "dev", steps[0])
    got = swap(send, "dev", steps[0])
    levels = len(steps) - 1
    sums = sums.reshape((2,) + (2,) * levels + (query_count, LANES))
    for level, bit in enumerate(steps[1:]):
        sums = sums + jnp.flip(swap(sums, "dev", bit), axis=1 + level)
    sums = sums.reshape(2, all_queries // 2, LANES)
    quarter = half_rows // 2
    send, rest = call(
        functools.partial(merge_body, length=length),
        [shape((quarter, width), BF16), shape((quarter, width), F32)],
        "merge",
    )(keep, got, sums)
    for bit in steps[1:-1]:
        rest = rest + swap(send, "dev", bit).astype(F32)
        quarter = quarter // 2
        rest, send = rest[:quarter], rest[quarter:].astype(BF16)
    got = swap(send, "dev", steps[-1])
    grad, loss = call(
        functools.partial(last_body, length=length),
        [shape(queries.shape, F32), shape((query_count, LANES), F32)],
        "last",
    )(queries, rest, got, sums[:, :query_count])
    return loss[:, 0], grad


def solution(mesh):
    placed = (
        P(("group", "dev"), None, None),
        P(("group", "dev"), None, None),
        P(("group", "dev"), None),
        P(),
    )
    return jax.shard_map(
        local,
        mesh=mesh,
        in_specs=placed,
        out_specs=(P(("group", "dev")), P(("group", "dev"), None, None)),
        check_vma=False,
    )
```

```python
import functools

import jax
import jax.numpy as jnp
from jax import lax
from jax.experimental import pallas as pl
from jax.experimental.pallas import tpu as pltpu
from jax.sharding import PartitionSpec as P

SOFTNESS = 0.02
EPSILON = 1e-06
LANES = 128
TAIL = 16
BASE = 256
UNROLL = 16
CHUNKS = 2
F32 = jnp.float32
BF16 = jnp.bfloat16


def call(body, out_shape, name, flops=0, in_specs=None, aliases={}):
    kwargs = {} if in_specs is None else {"in_specs": in_specs}
    return pl.pallas_call(
        body,
        out_shape=out_shape,
        input_output_aliases=aliases,
        name=name,
        cost_estimate=pl.CostEstimate(flops=flops, bytes_accessed=1 << 20, transcendentals=0),
        compiler_params=pltpu.CompilerParams(vmem_limit_bytes=48 * 1024 * 1024),
        **kwargs,
    )


def unit(values):
    floats = values.astype(F32)
    scale = lax.rsqrt(jnp.sum(floats * floats, axis=-1, keepdims=True) + EPSILON)
    return floats * scale, scale


def pack_body(queries_ref, cand_ref, out_ref):
    count, length, width = queries_ref.shape
    rows = count * length
    out_ref[:rows] = unit(queries_ref[...])[0].astype(BF16).reshape(rows, width)
    ids = jnp.broadcast_to(cand_ref[...], (TAIL, LANES))
    high = ids // BASE
    low = ids - high * BASE
    place = lax.broadcasted_iota(jnp.int32, (TAIL, LANES), 0)
    digits = jnp.where(place == 0, high, jnp.where(place == 1, low, 0))
    out_ref[rows:] = digits.astype(F32).astype(BF16)


def unit_body(passages_ref, out_ref):
    def step(index, carry):
        out_ref[index] = unit(passages_ref[index])[0].astype(BF16)
        return carry

    lax.fori_loop(0, passages_ref.shape[0], step, 0)


def route_body(docs_ref, pay_ref, out_ref, *, rows, pieces):
    blocks = pay_ref.shape[0]
    parts = out_ref.shape[1] - 1
    ids = []
    for block in range(blocks):
        tile = pay_ref[block, rows : rows + TAIL].astype(F32)
        ids.append((tile[0:1] * BASE + tile[1:2]).astype(jnp.int32))
    ids = jnp.concatenate(ids, axis=0)
    pair = lax.broadcasted_iota(jnp.int32, (blocks, LANES), 0) * LANES
    pair = pair + lax.broadcasted_iota(jnp.int32, (blocks, LANES), 1)
    upper = lax.broadcasted_iota(jnp.int32, (LANES, LANES), 0)
    lane = lax.broadcasted_iota(jnp.int32, (LANES, LANES), 1)
    triangle = (upper <= lane).astype(F32)
    diagonal = upper == lane
    place = lax.broadcasted_iota(jnp.int32, (parts * LANES, LANES), 0).astype(F32)
    for piece, (start, size) in enumerate(pieces):
        local = jnp.full((blocks, LANES), -1, jnp.int32)
        for index in range(size):
            local = jnp.where(ids == docs_ref[start + index], index, local)
        mask = local >= 0
        code = (local * (blocks * LANES) + pair).astype(F32)
        ranks = jnp.dot(mask.astype(F32), triangle, preferred_element_type=F32)
        before = jnp.zeros((1, 1), F32)
        found = jnp.zeros((parts * LANES, LANES), F32)
        for block in range(blocks):
            row = ranks[block : block + 1]
            slot = jnp.where(mask[block : block + 1], before + row - 1.0, -1.0)
            found = found + jnp.where(place == slot, code[block : block + 1], 0.0)
            before = before + row[:, LANES - 1 : LANES]
        packed = jnp.sum(found, axis=1, keepdims=True)
        for part in range(parts):
            value = packed[part * LANES : (part + 1) * LANES]
            line = jnp.sum(jnp.where(diagonal, value, 0.0), axis=0, keepdims=True)
            out_ref[piece, part : part + 1] = line.astype(jnp.int32)
        out_ref[piece, parts : parts + 1] = jnp.broadcast_to(before, (1, LANES)).astype(jnp.int32)


def score_pairs(piece, list_ref, pay_ref, pass_ref, acc_ref, sums_ref, length, list_len):
    parts = list_ref.shape[1] - 1
    blocks = pay_ref.shape[0]
    per_block = LANES // list_len
    queries = blocks * per_block
    quarter = queries // 4
    count = list_ref[piece, parts, 0]

    def step(index, carry):
        pairs = []
        for offset in range(UNROLL):
            slot = index * UNROLL + offset
            code = list_ref[piece, slot // LANES, slot % LANES]
            pair = code % (blocks * LANES)
            query = pair // list_len
            weight = jnp.where(slot < count, 1.0, 0.0).astype(F32)
            row = pl.multiple_of((query % per_block) * length, length)
            tokens = pay_ref[query // per_block, pl.ds(row, length)]
            passage = pass_ref[code // (blocks * LANES)]
            pairs.append((query, (pair % list_len) == 0, weight, tokens, passage))
        contract = (((1,), (1,)), ((), ()))
        logits = [
            lax.dot_general(tokens, passage, contract, preferred_element_type=F32)
            for _, _, _, tokens, passage in pairs
        ]
        terms = [jnp.exp(block * (1.0 / SOFTNESS)) for block in logits]
        masses = [jnp.sum(block, axis=1, keepdims=True) for block in terms]
        pulled = [
            jnp.dot(block.astype(BF16), pair[4], preferred_element_type=F32)
            for block, pair in zip(terms, pairs)
        ]
        done = []
        for (query, first, weight, _, _), mass, rows in zip(pairs, masses, pulled):
            score = SOFTNESS * jnp.sum(jnp.log(mass), axis=0, keepdims=True)
            exp_score = jnp.exp(score)
            region = query // quarter
            moved = ((region % 2) * 2 + region // 2) * quarter + query % quarter
            target = jnp.where(first, queries + moved, query)
            factor = jnp.where(first, 1.0, exp_score) * weight
            value = jnp.where(first, score, exp_score) * weight
            entry = jnp.where(first, queries, 0) + query
            done.append((target, (rows / mass) * factor, entry, value))
        for target, product, entry, value in done:
            at = pl.ds(pl.multiple_of(target * length, length), length)
            acc_ref[at] = acc_ref[at] + product
            sums_ref[pl.ds(entry, 1)] = sums_ref[pl.ds(entry, 1)] + value
        return carry

    lax.fori_loop(0, (count + UNROLL - 1) // UNROLL, step, 0)


def first_score_body(list_ref, pay_ref, pass_ref, acc_ref, sums_ref, *, piece, **sizes):
    acc_ref[...] = jnp.zeros_like(acc_ref)
    sums_ref[...] = jnp.zeros_like(sums_ref)
    score_pairs(piece, list_ref, pay_ref, pass_ref, acc_ref, sums_ref, **sizes)


def score_body(list_ref, pay_ref, pass_ref, _, __, acc_ref, sums_ref, *, piece, **sizes):
    score_pairs(piece, list_ref, pay_ref, pass_ref, acc_ref, sums_ref, **sizes)


def last_score_body(
    list_ref, pay_ref, pass_ref, _, __, acc_ref, sums_ref, others_ref, firsts_ref, *, piece, **sizes
):
    score_pairs(piece, list_ref, pay_ref, pass_ref, acc_ref, sums_ref, **sizes)
    half = others_ref.shape[0]
    others_ref[...] = acc_ref[half : 2 * half].astype(BF16)
    firsts_ref[...] = acc_ref[3 * half : 4 * half].astype(BF16)


def halve_body(acc_ref, others_ref, firsts_ref, send_a, send_b, keep_a, keep_b):
    half = others_ref.shape[0]
    quarter = half // 2
    for start, got, send, keep in (
        (0, others_ref, send_a, keep_a),
        (2 * half, firsts_ref, send_b, keep_b),
    ):
        keep[...] = acc_ref[start : start + quarter] + got[:quarter].astype(F32)
        rest = acc_ref[start + quarter : start + half] + got[quarter:].astype(F32)
        send[...] = rest.astype(BF16)


def merge_body(others_ref, got_others, firsts_ref, got_firsts, sums_ref, send_ref, rest_ref, *, length):
    queries = sums_ref.shape[1]

    def part(index):
        at = slice(index * length, (index + 1) * length)
        others = others_ref[at] + got_others[at].astype(F32)
        first = firsts_ref[at] + got_firsts[at].astype(F32)
        return others - sums_ref[0, index : index + 1] * first

    for index in range(queries // 2):
        at = slice(index * length, (index + 1) * length)
        rest_ref[at] = part(index)
        send_ref[at] = part(index + queries // 2).astype(BF16)


def last_body(queries_ref, keep_ref, got_ref, sums_ref, grad_ref, loss_ref, *, length):
    for index in range(queries_ref.shape[0]):
        at = slice(index * length, (index + 1) * length)
        spread = sums_ref[0, index : index + 1]
        score = sums_ref[1, index : index + 1]
        total = spread + jnp.exp(score)
        loss_ref[index : index + 1] = jnp.log(total) - score
        gradient = (keep_ref[at] + got_ref[at].astype(F32)) / total
        query_unit, query_scale = unit(queries_ref[index])
        along = jnp.sum(query_unit * gradient, axis=-1, keepdims=True)
        grad_ref[index] = (gradient - query_unit * along) * query_scale


def swap(value, axis, bit):
    size = lax.axis_size(axis)
    return lax.ppermute(value, axis, [(index, index ^ bit) for index in range(size)])


def bits_of(size):
    return [1 << power for power in reversed(range(size.bit_length() - 1))]


def spread_offsets(size):
    offsets = [0]
    for bit in bits_of(size):
        offsets = offsets + [offset ^ bit for offset in offsets]
    return offsets


def spread(block):
    blocks = [block]
    for bit in bits_of(lax.axis_size("group") // 2):
        blocks = blocks + [swap(held, "group", bit) for held in blocks]
    return blocks


def local(queries, passages, candidates, location):
    group_count = lax.axis_size("group")
    dev_count = lax.axis_size("dev")
    device_total = group_count * dev_count
    query_count, length, width = queries.shape
    pass_count, pass_len, _ = passages.shape
    list_len = candidates.shape[1]
    pair_count = query_count * list_len
    rows = query_count * length
    slot_cap = max(2, (3 * pair_count + device_total - 1) // device_total)
    group = lax.axis_index("group")
    dev = lax.axis_index("dev")
    shape = jax.ShapeDtypeStruct

    half_bit = group_count // 2
    chunk = pass_count // CHUNKS
    far_raw = [
        swap(passages[start : start + chunk], "group", half_bit)
        for start in range(0, pass_count, chunk)
    ]
    payload = call(pack_body, shape((rows + TAIL, width), BF16), "query_units")(
        queries, candidates.reshape(1, pair_count)
    )
    units = call(unit_body, shape(passages.shape, BF16), "passage_units")(passages)
    held = spread(units)
    near_offsets = spread_offsets(half_bit)
    pieces = [(offset, 0, pass_count) for offset in near_offsets]
    pieces += [
        (offset ^ half_bit, start, chunk)
        for start in range(0, pass_count, chunk)
        for offset in near_offsets
    ]
    held_rows = jnp.concatenate(
        [
            ((group ^ offset) * dev_count + dev) * pass_count + start + jnp.arange(size)
            for offset, start, size in pieces
        ]
    )
    hits = location[None, :] == held_rows.astype(jnp.int32)[:, None]
    documents = jnp.arange(location.shape[0], dtype=jnp.int32)
    docs = jnp.sum(jnp.where(hits, documents[None, :], 0), axis=1)

    pay = payload[None]
    for bit in bits_of(dev_count):
        pay = jnp.concatenate([pay, swap(pay, "dev", bit)], axis=0)

    parts = -(-dev_count * min(pair_count, slot_cap) // LANES)
    starts = [sum(piece[2] for piece in pieces[:index]) for index in range(len(pieces))]
    spans = tuple((start, piece[2]) for start, piece in zip(starts, pieces))
    smem, vmem = (pl.BlockSpec(memory_space=space) for space in (pltpu.SMEM, pltpu.VMEM))
    lists = call(
        functools.partial(route_body, rows=rows, pieces=spans),
        shape((len(pieces), parts + 1, LANES), jnp.int32),
        "route",
        in_specs=[smem, vmem],
    )(docs, pay)

    all_queries = dev_count * query_count
    half_rows = all_queries * length // 2
    totals = [shape((4 * half_rows, width), F32), shape((2 * all_queries, LANES), F32)]
    sends = [shape((half_rows, width), BF16)] * 2
    state = None
    piece = 0

    def score(block, last=False):
        body = first_score_body if state is None else last_score_body if last else score_body
        return call(
            functools.partial(body, piece=piece, length=length, list_len=list_len),
            totals + (sends if last else []),
            "score",
            all_queries * list_len // len(pieces) * length * pass_len * width * 4,
            [smem, vmem, vmem] + ([] if state is None else [vmem, vmem]),
            aliases={} if state is None else {3: 0, 4: 1},
        )(lists, pay, block, *(state or ()))

    for block in held:
        state = score(block)
        piece += 1
    for index, raw in enumerate(far_raw):
        raw, *state = lax.optimization_barrier((raw, *state))
        block_units = call(unit_body, shape(raw.shape, BF16), "passage_units")(raw)
        for block in spread(block_units):
            state = score(block, piece == len(pieces) - 1)[: 4 if piece == len(pieces) - 1 else 2]
            piece += 1
    acc, sums, others, firsts = state

    steps = bits_of(dev_count)[::-1]
    got_others = swap(others, "dev", steps[0])
    got_firsts = swap(firsts, "dev", steps[1])
    sums = sums.reshape((2, 2, all_queries // 2, LANES))
    sums = sums[:, 0] + swap(sums[:, 1], "dev", steps[0])
    sums = sums.reshape((2, 2, all_queries // 4, LANES))
    sums = sums[:, 0] + swap(sums[:, 1], "dev", steps[1])
    levels = len(steps) - 2
    sums = sums.reshape((2,) + (2,) * levels + (query_count, LANES))
    for level, bit in enumerate(steps[2:]):
        sums = sums + jnp.flip(swap(sums, "dev", bit), axis=1 + level)
    sums = sums.reshape(2, all_queries // 4, LANES)
    quarter = half_rows // 2
    send_others, send_firsts, others, firsts = call(
        halve_body, [shape((quarter, width), BF16)] * 2 + [shape((quarter, width), F32)] * 2, "halve"
    )(acc, got_others, got_firsts)
    got_others = swap(send_others, "dev", steps[1])
    got_firsts = swap(send_firsts, "dev", steps[0])
    quarter = quarter // 2
    send, rest = call(
        functools.partial(merge_body, length=length),
        [shape((quarter, width), BF16), shape((quarter, width), F32)],
        "merge",
    )(others, got_others, firsts, got_firsts, sums)
    for bit in steps[2:-1]:
        rest = rest + swap(send, "dev", bit).astype(F32)
        quarter = quarter // 2
        rest, send = rest[:quarter], rest[quarter:].astype(BF16)
    got = swap(send, "dev", steps[-1])
    grad, loss = call(
        functools.partial(last_body, length=length),
        [shape(queries.shape, F32), shape((query_count, LANES), F32)],
        "last",
    )(queries, rest, got, sums[:, :query_count])
    return loss[:, 0], grad


def solution(mesh):
    placed = (
        P(("group", "dev"), None, None),
        P(("group", "dev"), None, None),
        P(("group", "dev"), None),
        P(),
    )
    return jax.shard_map(
        local,
        mesh=mesh,
        in_specs=placed,
        out_specs=(P(("group", "dev")), P(("group", "dev"), None, None)),
        check_vma=False,
    )
```

```python
import functools

import jax
import jax.numpy as jnp
from jax import lax
from jax.experimental import pallas as pl
from jax.experimental.pallas import tpu as pltpu
from jax.sharding import PartitionSpec as P

SOFTNESS = 0.02
EPSILON = 1e-06
LANES = 128
TAIL = 16
BASE = 256
UNROLL = 16
SHIFT = 1 << 16
F32 = jnp.float32
BF16 = jnp.bfloat16


def call(body, out_shape, name, in_specs=None, aliases={}):
    kwargs = {} if in_specs is None else {"in_specs": in_specs}
    return pl.pallas_call(
        body,
        out_shape=out_shape,
        input_output_aliases=aliases,
        name=name,
        cost_estimate=pl.CostEstimate(flops=0, bytes_accessed=0, transcendentals=0),
        compiler_params=pltpu.CompilerParams(vmem_limit_bytes=48 * 1024 * 1024),
        **kwargs,
    )


def unit(values):
    floats = values.astype(F32)
    scale = lax.rsqrt(jnp.sum(floats * floats, axis=-1, keepdims=True) + EPSILON)
    return floats * scale, scale


def pack_body(queries_ref, cand_ref, out_ref):
    count, length, width = queries_ref.shape
    rows = count * length
    out_ref[:rows] = unit(queries_ref[...])[0].astype(BF16).reshape(rows, width)
    ids = jnp.concatenate([cand_ref[index : index + 1] for index in range(count)], axis=1)
    ids = jnp.broadcast_to(ids, (TAIL, LANES))
    high = ids // BASE
    low = ids - high * BASE
    place = lax.broadcasted_iota(jnp.int32, (TAIL, LANES), 0)
    digits = jnp.where(place == 0, high, jnp.where(place == 1, low, 0))
    out_ref[rows:] = digits.astype(F32).astype(BF16)


def unit_body(*refs):
    half = len(refs) // 2
    for source, out_ref in zip(refs[:half], refs[half:]):
        count = source.shape[0]
        together = min(count, 8)

        def step(index, carry, source=source, out_ref=out_ref, together=together):
            for offset in range(together):
                at = index * together + offset
                out_ref[at] = unit(source[at])[0].astype(BF16)
            return carry

        lax.fori_loop(0, count // together, step, 0)


def route_body(docs_ref, *refs, rows, size, list_len):
    *pay_refs, out_ref, list_ref = refs
    per_ref = pay_refs[0].shape[0]
    blocks = per_ref * len(pay_refs)
    stride = rows + TAIL
    ids = []
    for index, pay_ref in enumerate(pay_refs):
        for block in range(per_ref):
            start = (index * per_ref + block) * stride
            out_ref[start : start + stride] = pay_ref[block]
            tile = pay_ref[block, rows:].astype(F32)
            ids.append((tile[0:1] * BASE + tile[1:2]).astype(jnp.int32))
    ids = jnp.concatenate(ids, axis=0)
    per_block = LANES // list_len
    queries = blocks * per_block
    block = lax.broadcasted_iota(jnp.int32, (blocks, LANES), 0)
    lane = lax.broadcasted_iota(jnp.int32, (blocks, LANES), 1)
    query = lane // list_len
    source = (block * stride + query * (rows // per_block)).astype(F32)
    quarter = blocks // 4
    region = block // quarter
    moved = block + jnp.where(region == 1, quarter, 0) - jnp.where(region == 2, quarter, 0)
    first = lane % list_len == 0
    target = jnp.where(first, queries + moved * per_block, block * per_block) + query
    target = (target - 2 * queries).astype(F32)
    upper = lax.broadcasted_iota(jnp.int32, (LANES, LANES), 0)
    column = lax.broadcasted_iota(jnp.int32, (LANES, LANES), 1)
    triangle = (upper <= column).astype(F32)
    diagonal = upper == column
    parts = list_ref.shape[2]
    place = lax.broadcasted_iota(jnp.int32, (parts * LANES, LANES), 0).astype(F32)
    for piece in range(list_ref.shape[0]):
        held = jnp.full((blocks, LANES), -1, jnp.int32)
        for index in range(size):
            held = jnp.where(ids == docs_ref[piece * size + index], index, held)
        mask = held >= 0
        code = held.astype(F32) * SHIFT + source
        ranks = jnp.dot(mask.astype(F32), triangle, preferred_element_type=F32)
        before = jnp.zeros((1, 1), F32)
        codes = jnp.zeros((parts * LANES, LANES), F32)
        targets = jnp.zeros((parts * LANES, LANES), F32)
        for index in range(blocks):
            row = ranks[index : index + 1]
            slot = jnp.where(mask[index : index + 1], before + row - 1.0, -1.0)
            here = place == slot
            codes = codes + jnp.where(here, code[index : index + 1], 0.0)
            targets = targets + jnp.where(here, target[index : index + 1], 0.0)
            before = before + row[:, LANES - 1 : LANES]
        for kind, found in enumerate((codes, targets + 2.0 * queries / LANES)):
            packed = jnp.sum(found, axis=1, keepdims=True)
            for part in range(parts):
                value = packed[part * LANES : (part + 1) * LANES]
                line = jnp.sum(jnp.where(diagonal, value, 0.0), axis=0, keepdims=True)
                list_ref[piece, kind, part : part + 1] = line.astype(jnp.int32)
        count = jnp.broadcast_to(before, (parts, LANES)).astype(jnp.int32)
        list_ref[piece, 2] = count


def score_pairs(piece, list_ref, pay_ref, pass_ref, acc_ref, sums_ref, length):
    queries = sums_ref.shape[0] // 2
    count = list_ref[piece, 2, 0, 0]
    contract = (((1,), (1,)), ((), ()))

    def step(index, carry):
        pairs = []
        for offset in range(UNROLL):
            slot = index * UNROLL + offset
            part, lane = lax.shift_right_logical(slot, 7), slot & (LANES - 1)
            code = list_ref[piece, 0, part, lane]
            row = pl.multiple_of(code & (SHIFT - 1), 16)
            passage = pass_ref[lax.shift_right_logical(code, SHIFT.bit_length() - 1)]
            pairs.append((list_ref[piece, 1, part, lane], pay_ref[pl.ds(row, length)], passage))
        logits = [
            lax.dot_general(tokens, passage, contract, preferred_element_type=F32)
            for _, tokens, passage in pairs
        ]
        terms = [jnp.exp(block * (1.0 / SOFTNESS)) for block in logits]
        masses = [jnp.sum(block, axis=1, keepdims=True) for block in terms]
        pulled = [
            jnp.dot(block.astype(BF16), pair[2], preferred_element_type=F32)
            for block, pair in zip(terms, pairs)
        ]
        done = []
        for (target, _, _), mass, rows in zip(pairs, masses, pulled):
            score = SOFTNESS * jnp.sum(jnp.log(mass), axis=0, keepdims=True)
            exp_score = jnp.exp(score)
            first = target >= queries
            factor = jnp.where(first, 1.0, exp_score)
            done.append((target, rows * (factor / mass), jnp.where(first, score, exp_score)))
        for target, product, value in done:
            at = pl.ds(pl.multiple_of(target * length, length), length)
            acc_ref[at] = acc_ref[at] + product
            sums_ref[pl.ds(target, 1)] = sums_ref[pl.ds(target, 1)] + value
        return carry

    lax.fori_loop(0, lax.div(count + UNROLL - 1, UNROLL), step, 0)


def near_score_body(list_ref, pay_ref, *refs, length):
    *pass_refs, acc_ref, sums_ref = refs
    acc_ref[...] = jnp.zeros_like(acc_ref)
    sums_ref[...] = jnp.zeros_like(sums_ref)
    for piece, pass_ref in enumerate(pass_refs):
        score_pairs(piece, list_ref, pay_ref, pass_ref, acc_ref, sums_ref, length)


def score_body(list_ref, pay_ref, pass_ref, _, __, acc_ref, sums_ref, *, piece, length):
    score_pairs(piece, list_ref, pay_ref, pass_ref, acc_ref, sums_ref, length)


def last_score_body(
    list_ref, pay_ref, pass_ref, _, __, acc_ref, sums_ref, others_ref, firsts_ref, *, piece, length
):
    score_pairs(piece, list_ref, pay_ref, pass_ref, acc_ref, sums_ref, length)
    half = others_ref.shape[0]
    others_ref[...] = acc_ref[half : 2 * half].astype(BF16)
    firsts_ref[...] = acc_ref[3 * half : 4 * half].astype(BF16)


def halve_body(acc_ref, others_ref, firsts_ref, send_a, send_b, keep_a, keep_b):
    half = others_ref.shape[0]
    quarter = half // 2
    for start, got, send, keep in (
        (0, others_ref, send_a, keep_a),
        (2 * half, firsts_ref, send_b, keep_b),
    ):
        keep[...] = acc_ref[start : start + quarter] + got[:quarter].astype(F32)
        rest = acc_ref[start + quarter : start + half] + got[quarter:].astype(F32)
        send[...] = rest.astype(BF16)


def merge_body(others_ref, got_others, firsts_ref, got_firsts, sums_ref, send_ref, rest_ref, *, length):
    queries = sums_ref.shape[1]

    def part(index):
        at = slice(index * length, (index + 1) * length)
        others = others_ref[at] + got_others[at].astype(F32)
        first = firsts_ref[at] + got_firsts[at].astype(F32)
        return others - sums_ref[0, index : index + 1] * first

    for index in range(queries // 2):
        at = slice(index * length, (index + 1) * length)
        rest_ref[at] = part(index)
        send_ref[at] = part(index + queries // 2).astype(BF16)


def last_body(queries_ref, keep_ref, got_ref, sums_ref, grad_ref, loss_ref, *, length):
    count = queries_ref.shape[0]
    losses = []
    for index in range(count):
        at = slice(index * length, (index + 1) * length)
        spread = sums_ref[0, index : index + 1]
        score = sums_ref[1, index : index + 1]
        total = spread + jnp.exp(score)
        losses.append(jnp.log(total) - score)
        gradient = (keep_ref[at] + got_ref[at].astype(F32)) / total
        query_unit, query_scale = unit(queries_ref[index])
        along = jnp.sum(query_unit * gradient, axis=-1, keepdims=True)
        grad_ref[index] = (gradient - query_unit * along) * query_scale
    losses = jnp.concatenate(losses, axis=0)
    place = lax.broadcasted_iota(jnp.int32, (count, LANES), 0)
    lane = lax.broadcasted_iota(jnp.int32, (count, LANES), 1)
    loss_ref[...] = jnp.sum(jnp.where(place == lane, losses, 0.0), axis=0, keepdims=True)[:, :count]


def swap(value, axis, bit):
    size = lax.axis_size(axis)
    return lax.ppermute(value, axis, [(index, index ^ bit) for index in range(size)])


def bits_of(size):
    return [1 << power for power in reversed(range(size.bit_length() - 1))]


def spread_offsets(size):
    offsets = [0]
    for bit in bits_of(size):
        offsets = offsets + [offset ^ bit for offset in offsets]
    return offsets


def spread(block):
    blocks = [block]
    for bit in bits_of(lax.axis_size("group") // 2):
        blocks = blocks + [swap(held, "group", bit) for held in blocks]
    return blocks


def local(queries, passages, candidates, location):
    group_count = lax.axis_size("group")
    dev_count = lax.axis_size("dev")
    device_total = group_count * dev_count
    query_count, length, width = queries.shape
    pass_count, pass_len, _ = passages.shape
    list_len = candidates.shape[1]
    pair_count = query_count * list_len
    rows = query_count * length
    slot_cap = max(2, (3 * pair_count + device_total - 1) // device_total)
    group = lax.axis_index("group")
    dev = lax.axis_index("dev")
    shape = jax.ShapeDtypeStruct

    half_bit = group_count // 2
    far_raw = swap(passages, "group", half_bit)
    near_raw = spread(passages)
    payload = call(pack_body, shape((rows + TAIL, width), BF16), "query_units")(queries, candidates)

    *first_bits, low, lowest = bits_of(dev_count)
    pay = payload[None]
    for bit in first_bits:
        pay = jnp.concatenate([pay, swap(pay, "dev", bit)], axis=0)
    pay_low = swap(pay, "dev", low)
    pays = [pay, pay_low, swap(pay, "dev", lowest), swap(pay_low, "dev", lowest)]

    near_offsets = spread_offsets(half_bit)
    offsets = near_offsets + [offset ^ half_bit for offset in near_offsets]
    held_rows = jnp.concatenate(
        [
            ((group ^ offset) * dev_count + dev) * pass_count + jnp.arange(pass_count)
            for offset in offsets
        ]
    )
    hits = location[None, :] == held_rows.astype(jnp.int32)[:, None]
    documents = jnp.arange(location.shape[0], dtype=jnp.int32)
    docs = jnp.sum(jnp.where(hits, documents[None, :], 0), axis=1)

    parts = -(-dev_count * min(pair_count, slot_cap) // LANES)
    smem, vmem = (pl.BlockSpec(memory_space=space) for space in (pltpu.SMEM, pltpu.VMEM))
    pay, lists = call(
        functools.partial(route_body, rows=rows, size=pass_count, list_len=list_len),
        [
            shape((dev_count * (rows + TAIL), width), BF16),
            shape((len(offsets), 3, parts, LANES), jnp.int32),
        ],
        "route",
        in_specs=[smem] + [vmem] * len(pays),
    )(docs, *pays)

    all_queries = dev_count * query_count
    half_rows = all_queries * length // 2
    totals = [
        shape(((2 * all_queries + 1) * length, width), F32),
        shape((2 * all_queries + 1, LANES), F32),
    ]
    sends = [shape((half_rows, width), BF16)] * 2
    near = call(unit_body, [shape(passages.shape, BF16)] * len(near_raw), "passage_units")(*near_raw)
    state = call(
        functools.partial(near_score_body, length=length),
        totals,
        "score_near",
        in_specs=[smem] + [vmem] * (1 + len(near)),
    )(lists, pay, *near)
    far_raw, *state = lax.optimization_barrier((far_raw, *state))
    far = spread(call(unit_body, shape(passages.shape, BF16), "passage_units")(far_raw))
    for index, held in enumerate(far):
        last = index == len(far) - 1
        state = call(
            functools.partial(
                last_score_body if last else score_body, piece=len(near) + index, length=length
            ),
            totals + (sends if last else []),
            "score_far",
            in_specs=[smem] + [vmem] * 4,
            aliases={3: 0, 4: 1},
        )(lists, pay, held, *state)
    acc, sums, others, firsts = state

    steps = bits_of(dev_count)[::-1]
    got_others = swap(others, "dev", steps[0])
    got_firsts = swap(firsts, "dev", steps[1])
    sums = sums[: 2 * all_queries].reshape(2, 2, 2, all_queries // 4, LANES)
    spreads, scores = sums[0], jnp.swapaxes(sums[1], 0, 1)
    sums = jnp.stack([spreads[0], scores[0]])
    sums = sums + swap(jnp.stack([spreads[1], scores[1]]), "dev", steps[0])
    sums = sums[:, 0] + swap(sums[:, 1], "dev", steps[1])
    levels = len(steps) - 2
    sums = sums.reshape((2,) + (2,) * levels + (query_count, LANES))
    for level, bit in enumerate(steps[2:]):
        sums = sums + jnp.flip(swap(sums, "dev", bit), axis=1 + level)
    sums = sums.reshape(2, all_queries // 4, LANES)
    quarter = half_rows // 2
    send_others, send_firsts, others, firsts = call(
        halve_body, [shape((quarter, width), BF16)] * 2 + [shape((quarter, width), F32)] * 2, "halve"
    )(acc, got_others, got_firsts)
    got_others = swap(send_others, "dev", steps[1])
    got_firsts = swap(send_firsts, "dev", steps[0])
    quarter = quarter // 2
    send, rest = call(
        functools.partial(merge_body, length=length),
        [shape((quarter, width), BF16), shape((quarter, width), F32)],
        "merge",
    )(others, got_others, firsts, got_firsts, sums)
    for bit in steps[2:-1]:
        rest = rest + swap(send, "dev", bit).astype(F32)
        quarter = quarter // 2
        rest, send = rest[:quarter], rest[quarter:].astype(BF16)
    got = swap(send, "dev", steps[-1])
    grad, loss = call(
        functools.partial(last_body, length=length),
        [shape(queries.shape, F32), shape((1, query_count), F32)],
        "last",
    )(queries, rest, got, sums[:, :query_count])
    return loss.reshape(query_count), grad


def solution(mesh):
    placed = (
        P(("group", "dev"), None, None),
        P(("group", "dev"), None, None),
        P(("group", "dev"), None),
        P(),
    )
    return jax.shard_map(
        local,
        mesh=mesh,
        in_specs=placed,
        out_specs=(P(("group", "dev")), P(("group", "dev"), None, None)),
        check_vma=False,
    )
```

```python
import functools

import jax
import jax.numpy as jnp
from jax import lax
from jax.experimental import pallas as pl
from jax.experimental.pallas import tpu as pltpu
from jax.sharding import PartitionSpec as P

SOFTNESS = 0.02
EPSILON = 1e-06
LANES = 128
TAIL = 16
BASE = 256
UNROLL = 16
SHIFT = 1 << 16
F32 = jnp.float32
BF16 = jnp.bfloat16


def call(body, out_shape, name, in_specs=None, aliases={}, scratch=(), cost=0):
    kwargs = {} if in_specs is None else {"in_specs": in_specs}
    return pl.pallas_call(
        body,
        out_shape=out_shape,
        input_output_aliases=aliases,
        scratch_shapes=list(scratch),
        name=name,
        cost_estimate=pl.CostEstimate(flops=0, bytes_accessed=cost, transcendentals=0),
        compiler_params=pltpu.CompilerParams(vmem_limit_bytes=20 * 1024 * 1024),
        **kwargs,
    )


def unit(values):
    floats = values.astype(F32)
    scale = lax.rsqrt(jnp.sum(floats * floats, axis=-1, keepdims=True) + EPSILON)
    return floats * scale, scale


def pack_body(queries_ref, cand_ref, out_ref):
    count, length, width = queries_ref.shape
    rows = count * length
    out_ref[:rows] = unit(queries_ref[...])[0].astype(BF16).reshape(rows, width)
    ids = jnp.concatenate([cand_ref[index : index + 1] for index in range(count)], axis=1)
    ids = jnp.broadcast_to(ids, (TAIL, LANES))
    high = ids // BASE
    low = ids - high * BASE
    place = lax.broadcasted_iota(jnp.int32, (TAIL, LANES), 0)
    digits = jnp.where(place == 0, high, jnp.where(place == 1, low, 0))
    out_ref[rows:] = digits.astype(F32).astype(BF16)


def turn_units(source, units_ref, turned_ref):
    count = source.shape[0]
    together = min(count, 8)

    def step(index, carry):
        for offset in range(together):
            at = index * together + offset
            units = unit(source[at])[0].astype(BF16)
            units_ref[at] = units
            turned_ref[at] = units.T
        return carry

    lax.fori_loop(0, count // together, step, 0)


def unit_body(*refs):
    half = len(refs) // 3
    for index, source in enumerate(refs[:half]):
        turn_units(source, refs[half + 2 * index], refs[half + 2 * index + 1])


def route_body(docs_ref, *refs, rows, size, list_len):
    *pay_refs, out_ref, list_ref = refs
    per_ref = pay_refs[0].shape[0]
    blocks = per_ref * len(pay_refs)
    stride = rows + TAIL
    ids = []
    for index, pay_ref in enumerate(pay_refs):
        for block in range(per_ref):
            start = (index * per_ref + block) * stride
            out_ref[start : start + stride] = pay_ref[block]
            tile = pay_ref[block, rows:].astype(F32)
            ids.append((tile[0:1] * BASE + tile[1:2]).astype(jnp.int32))
    ids = jnp.concatenate(ids, axis=0)
    per_block = LANES // list_len
    queries = blocks * per_block
    block = lax.broadcasted_iota(jnp.int32, (blocks, LANES), 0)
    lane = lax.broadcasted_iota(jnp.int32, (blocks, LANES), 1)
    query = lane // list_len
    source = (block * stride + query * (rows // per_block)).astype(F32)
    quarter = blocks // 4
    region = block // quarter
    moved = block + jnp.where(region == 1, quarter, 0) - jnp.where(region == 2, quarter, 0)
    first = lane % list_len == 0
    target = jnp.where(first, queries + moved * per_block, block * per_block) + query
    target = (target - 2 * queries).astype(F32)
    upper = lax.broadcasted_iota(jnp.int32, (LANES, LANES), 0)
    column = lax.broadcasted_iota(jnp.int32, (LANES, LANES), 1)
    triangle = (upper <= column).astype(F32)
    diagonal = upper == column
    parts = list_ref.shape[2]
    place = lax.broadcasted_iota(jnp.int32, (parts * LANES, LANES), 0).astype(F32)
    for piece in range(list_ref.shape[0]):
        held = jnp.full((blocks, LANES), -1, jnp.int32)
        for index in range(size):
            held = jnp.where(ids == docs_ref[piece * size + index], index, held)
        mask = held >= 0
        code = held.astype(F32) * SHIFT + source
        ranks = jnp.dot(mask.astype(F32), triangle, preferred_element_type=F32)
        before = jnp.zeros((1, 1), F32)
        codes = jnp.zeros((parts * LANES, LANES), F32)
        targets = jnp.zeros((parts * LANES, LANES), F32)
        for index in range(blocks):
            row = ranks[index : index + 1]
            slot = jnp.where(mask[index : index + 1], before + row - 1.0, -1.0)
            here = place == slot
            codes = codes + jnp.where(here, code[index : index + 1], 0.0)
            targets = targets + jnp.where(here, target[index : index + 1], 0.0)
            before = before + row[:, LANES - 1 : LANES]
        for kind, found in enumerate((codes, targets + 2.0 * queries / LANES)):
            packed = jnp.sum(found, axis=1, keepdims=True)
            for part in range(parts):
                value = packed[part * LANES : (part + 1) * LANES]
                line = jnp.sum(jnp.where(diagonal, value, 0.0), axis=0, keepdims=True)
                list_ref[piece, kind, part : part + 1] = line.astype(jnp.int32)
        count = jnp.broadcast_to(before, (parts, LANES)).astype(jnp.int32)
        list_ref[piece, 2] = count


def score_pairs(list_ref, pay_ref, pass_ref, turned_ref, acc_ref, sums_ref, length):
    queries = sums_ref.shape[0] // 2
    count = list_ref[2, 0, 0]

    def step(index, carry):
        pairs = []
        for offset in range(UNROLL):
            slot = index * UNROLL + offset
            part, lane = lax.shift_right_logical(slot, 7), slot & (LANES - 1)
            code = list_ref[0, part, lane]
            row = pl.multiple_of(code & (SHIFT - 1), 16)
            place = lax.shift_right_logical(code, SHIFT.bit_length() - 1)
            pairs.append((list_ref[1, part, lane], pay_ref[pl.ds(row, length)], place))
        logits = [
            jnp.dot(tokens, turned_ref[place], preferred_element_type=F32)
            for _, tokens, place in pairs
        ]
        terms = [jnp.exp(block * (1.0 / SOFTNESS)) for block in logits]
        masses = [jnp.sum(block, axis=1, keepdims=True) for block in terms]
        pulled = [
            jnp.dot(block.astype(BF16), pass_ref[pair[2]], preferred_element_type=F32)
            for block, pair in zip(terms, pairs)
        ]
        done = []
        for (target, _, _), mass, rows in zip(pairs, masses, pulled):
            score = SOFTNESS * jnp.sum(jnp.log(mass), axis=0, keepdims=True)
            exp_score = jnp.exp(score)
            first = target >= queries
            factor = jnp.where(first, 1.0, exp_score)
            done.append((target, rows * (factor / mass), jnp.where(first, score, exp_score)))
        for target, product, value in done:
            at = pl.ds(pl.multiple_of(target * length, length), length)
            acc_ref[at] = acc_ref[at] + product
            sums_ref[pl.ds(target, 1)] = sums_ref[pl.ds(target, 1)] + value
        return carry

    lax.fori_loop(0, lax.div(count + UNROLL - 1, UNROLL), step, 0)


def near_score_body(lists_ref, pay_ref, *refs, length):
    *pass_refs, acc_ref, sums_ref, list_ref, sem = refs
    move = pltpu.make_async_copy(lists_ref.at[: len(pass_refs) // 2], list_ref, sem)
    move.start()
    acc_ref[...] = jnp.zeros_like(acc_ref)
    sums_ref[...] = jnp.zeros_like(sums_ref)
    move.wait()
    for piece in range(len(pass_refs) // 2):
        score_pairs(
            list_ref.at[piece],
            pay_ref,
            pass_refs[2 * piece],
            pass_refs[2 * piece + 1],
            acc_ref,
            sums_ref,
            length,
        )


def far_score_body(lists_ref, pay_ref, raw_ref, _, __, acc_ref, sums_ref, *refs, piece, length):
    *send_refs, pass_ref, turned_ref, list_ref, sem = refs
    move = pltpu.make_async_copy(lists_ref.at[piece], list_ref, sem)
    move.start()
    turn_units(raw_ref, pass_ref, turned_ref)
    move.wait()
    score_pairs(list_ref, pay_ref, pass_ref, turned_ref, acc_ref, sums_ref, length)
    if send_refs:
        others_ref, firsts_ref = send_refs
        half = others_ref.shape[0]
        others_ref[...] = acc_ref[half : 2 * half].astype(BF16)
        firsts_ref[...] = acc_ref[3 * half : 4 * half].astype(BF16)


def halve_body(acc_ref, others_ref, firsts_ref, send_a, send_b, keep_a, keep_b):
    half = others_ref.shape[0]
    quarter = half // 2
    for start, got, send, keep in (
        (0, others_ref, send_a, keep_a),
        (2 * half, firsts_ref, send_b, keep_b),
    ):
        keep[...] = acc_ref[start : start + quarter] + got[:quarter].astype(F32)
        rest = acc_ref[start + quarter : start + half] + got[quarter:].astype(F32)
        send[...] = rest.astype(BF16)


def merge_body(others_ref, got_others, firsts_ref, got_firsts, sums_ref, send_ref, rest_ref, *, length):
    queries = sums_ref.shape[1]

    def part(index):
        at = slice(index * length, (index + 1) * length)
        others = others_ref[at] + got_others[at].astype(F32)
        first = firsts_ref[at] + got_firsts[at].astype(F32)
        return others - sums_ref[0, index : index + 1] * first

    for index in range(queries // 2):
        at = slice(index * length, (index + 1) * length)
        rest_ref[at] = part(index)
        send_ref[at] = part(index + queries // 2).astype(BF16)


def last_body(queries_ref, keep_ref, got_ref, sums_ref, grad_ref, loss_ref, *, length):
    count = queries_ref.shape[0]
    losses = []
    for index in range(count):
        at = slice(index * length, (index + 1) * length)
        spread = sums_ref[0, index : index + 1]
        score = sums_ref[1, index : index + 1]
        total = spread + jnp.exp(score)
        losses.append(jnp.log(total) - score)
        gradient = (keep_ref[at] + got_ref[at].astype(F32)) / total
        query_unit, query_scale = unit(queries_ref[index])
        along = jnp.sum(query_unit * gradient, axis=-1, keepdims=True)
        grad_ref[index] = (gradient - query_unit * along) * query_scale
    losses = jnp.concatenate(losses, axis=0)
    place = lax.broadcasted_iota(jnp.int32, (count, LANES), 0)
    lane = lax.broadcasted_iota(jnp.int32, (count, LANES), 1)
    loss_ref[...] = jnp.sum(jnp.where(place == lane, losses, 0.0), axis=0, keepdims=True)[:, :count]


def swap(value, axis, bit):
    size = lax.axis_size(axis)
    return lax.ppermute(value, axis, [(index, index ^ bit) for index in range(size)])


def bits_of(size):
    return [1 << power for power in reversed(range(size.bit_length() - 1))]


def spread_offsets(size):
    offsets = [0]
    for bit in bits_of(size):
        offsets = offsets + [offset ^ bit for offset in offsets]
    return offsets


def spread(block):
    blocks = [block]
    for bit in bits_of(lax.axis_size("group") // 2):
        blocks = blocks + [swap(held, "group", bit) for held in blocks]
    return blocks


def local(queries, passages, candidates, location):
    group_count = lax.axis_size("group")
    dev_count = lax.axis_size("dev")
    device_total = group_count * dev_count
    query_count, length, width = queries.shape
    pass_count, pass_len, _ = passages.shape
    list_len = candidates.shape[1]
    pair_count = query_count * list_len
    rows = query_count * length
    slot_cap = max(2, (3 * pair_count + device_total - 1) // device_total)
    group = lax.axis_index("group")
    dev = lax.axis_index("dev")
    shape = jax.ShapeDtypeStruct

    half_bit = group_count // 2
    far_raw = swap(passages, "group", half_bit)
    near_raw = spread(passages)
    hbm, smem, vmem = (
        pl.BlockSpec(memory_space=space) for space in (pltpu.HBM, pltpu.SMEM, pltpu.VMEM)
    )
    payload = call(
        pack_body,
        shape((rows + TAIL, width), BF16),
        "query_units",
        [vmem, vmem],
    )(queries, candidates)

    *first_bits, low, lowest = bits_of(dev_count)
    pay = payload[None]
    for bit in first_bits:
        pay = jnp.concatenate([pay, swap(pay, "dev", bit)], axis=0)
    turned = shape((pass_count, width, pass_len), BF16)
    near = call(unit_body, [shape(passages.shape, BF16), turned] * len(near_raw), "passage_units")(
        *near_raw
    )
    pay_low = swap(pay, "dev", low)
    pays = [pay, pay_low, swap(pay, "dev", lowest), swap(pay_low, "dev", lowest)]
    pays[3], near = lax.optimization_barrier((pays[3], near))

    near_offsets = spread_offsets(half_bit)
    offsets = near_offsets + [offset ^ half_bit for offset in near_offsets]
    held_rows = jnp.concatenate(
        [
            ((group ^ offset) * dev_count + dev) * pass_count + jnp.arange(pass_count)
            for offset in offsets
        ]
    )
    hits = location[None, :] == held_rows.astype(jnp.int32)[:, None]
    documents = jnp.arange(location.shape[0], dtype=jnp.int32)
    docs = jnp.sum(jnp.where(hits, documents[None, :], 0), axis=1)

    parts = -(-dev_count * min(pair_count, slot_cap) // LANES)
    pay, lists = call(
        functools.partial(route_body, rows=rows, size=pass_count, list_len=list_len),
        [
            shape((dev_count * (rows + TAIL), width), BF16),
            shape((len(offsets), 3, parts, LANES), jnp.int32),
        ],
        "route",
        in_specs=[smem] + [vmem] * len(pays),
    )(docs, *pays)

    all_queries = dev_count * query_count
    half_rows = all_queries * length // 2
    totals = [
        shape(((2 * all_queries + 1) * length, width), F32),
        shape((2 * all_queries + 1, LANES), F32),
    ]
    sends = [shape((half_rows, width), BF16)] * 2
    state = call(
        functools.partial(near_score_body, length=length),
        totals,
        "score_near",
        [vmem] * (2 + len(near)),
        scratch=[
            pltpu.SMEM((len(near_raw), 3, parts, LANES), jnp.int32),
            pltpu.SemaphoreType.DMA(()),
        ],
    )(lists, pay, *near)
    far_raw, *state = lax.optimization_barrier((far_raw, *state))
    far = spread(far_raw)
    for index, raw in enumerate(far):
        last = index == len(far) - 1
        state = call(
            functools.partial(far_score_body, piece=len(far) + index, length=length),
            totals + (sends if last else []),
            "score_far",
            [vmem] * 5,
            {3: 0, 4: 1},
            [
                pltpu.VMEM(passages.shape, BF16),
                pltpu.VMEM(turned.shape, BF16),
                pltpu.SMEM((3, parts, LANES), jnp.int32),
                pltpu.SemaphoreType.DMA(()),
            ],
        )(lists, pay, raw, *state)
    acc, sums, others, firsts = state

    steps = bits_of(dev_count)[::-1]
    got_others = swap(others, "dev", steps[0])
    got_firsts = swap(firsts, "dev", steps[1])
    sums = sums[: 2 * all_queries].reshape(2, 2, 2, all_queries // 4, LANES)
    spreads, scores = sums[0], jnp.swapaxes(sums[1], 0, 1)
    sums = jnp.stack([spreads[0], scores[0]])
    sums = sums + swap(jnp.stack([spreads[1], scores[1]]), "dev", steps[0])
    sums = sums[:, 0] + swap(sums[:, 1], "dev", steps[1])
    levels = len(steps) - 2
    sums = sums.reshape((2,) + (2,) * levels + (query_count, LANES))
    for level, bit in enumerate(steps[2:]):
        sums = sums + jnp.flip(swap(sums, "dev", bit), axis=1 + level)
    sums = sums.reshape(2, all_queries // 4, LANES)
    quarter = half_rows // 2
    send_others, send_firsts, others, firsts = call(
        halve_body, [shape((quarter, width), BF16)] * 2 + [shape((quarter, width), F32)] * 2, "halve"
    )(acc, got_others, got_firsts)
    got_others = swap(send_others, "dev", steps[1])
    got_firsts = swap(send_firsts, "dev", steps[0])
    quarter = quarter // 2
    send, rest = call(
        functools.partial(merge_body, length=length),
        [shape((quarter, width), BF16), shape((quarter, width), F32)],
        "merge",
    )(others, got_others, firsts, got_firsts, sums)
    for bit in steps[2:-1]:
        rest = rest + swap(send, "dev", bit).astype(F32)
        quarter = quarter // 2
        rest, send = rest[:quarter], rest[quarter:].astype(BF16)
    got = swap(send, "dev", steps[-1])
    grad, loss = call(
        functools.partial(last_body, length=length),
        [shape(queries.shape, F32), shape((1, query_count), F32)],
        "last",
    )(queries, rest, got, sums[:, :query_count])
    return loss.reshape(query_count), grad


def solution(mesh):
    placed = (
        P(("group", "dev"), None, None),
        P(("group", "dev"), None, None),
        P(("group", "dev"), None),
        P(),
    )
    return jax.shard_map(
        local,
        mesh=mesh,
        in_specs=placed,
        out_specs=(P(("group", "dev")), P(("group", "dev"), None, None)),
        check_vma=False,
    )
```

```python
import functools

import jax
import jax.numpy as jnp
from jax import lax
from jax.experimental import pallas as pl
from jax.experimental.pallas import tpu as pltpu
from jax.sharding import PartitionSpec as P

SOFTNESS = 0.02
EPSILON = 1e-06
LANES = 128
TAIL = 16
BASE = 256
UNROLL = 16
SHIFT = 1 << 16
F32 = jnp.float32
BF16 = jnp.bfloat16


def call(body, out_shape, name, in_specs=None, aliases={}, scratch=(), cost=0):
    kwargs = {} if in_specs is None else {"in_specs": in_specs}
    return pl.pallas_call(
        body,
        out_shape=out_shape,
        input_output_aliases=aliases,
        scratch_shapes=list(scratch),
        name=name,
        cost_estimate=pl.CostEstimate(flops=0, bytes_accessed=cost, transcendentals=0),
        compiler_params=pltpu.CompilerParams(vmem_limit_bytes=20 * 1024 * 1024),
        **kwargs,
    )


def unit(values):
    floats = values.astype(F32)
    scale = lax.rsqrt(jnp.sum(floats * floats, axis=-1, keepdims=True) + EPSILON)
    return floats * scale, scale


def pack_body(queries_ref, cand_ref, out_ref):
    count, length, width = queries_ref.shape
    rows = count * length
    out_ref[:rows] = unit(queries_ref[...])[0].astype(BF16).reshape(rows, width)
    ids = jnp.concatenate([cand_ref[index : index + 1] for index in range(count)], axis=1)
    ids = jnp.broadcast_to(ids, (TAIL, LANES))
    high = ids // BASE
    low = ids - high * BASE
    place = lax.broadcasted_iota(jnp.int32, (TAIL, LANES), 0)
    digits = jnp.where(place == 0, high, jnp.where(place == 1, low, 0))
    out_ref[rows:] = digits.astype(F32).astype(BF16)


def turn_units(source, units_ref, turned_ref):
    count = source.shape[0]
    together = min(count, 8)

    def step(index, carry):
        for offset in range(together):
            at = index * together + offset
            units = unit(source[at])[0].astype(BF16)
            units_ref[at] = units
            turned_ref[at] = units.T
        return carry

    lax.fori_loop(0, count // together, step, 0)


def unit_body(*refs):
    half = len(refs) // 3
    for index, source in enumerate(refs[:half]):
        turn_units(source, refs[half + 2 * index], refs[half + 2 * index + 1])


def route_body(docs_ref, *refs, rows, size, list_len):
    *pay_refs, out_ref, list_ref = refs
    per_ref = pay_refs[0].shape[0]
    blocks = per_ref * len(pay_refs)
    stride = rows + TAIL
    ids = []
    for index, pay_ref in enumerate(pay_refs):
        for block in range(per_ref):
            start = (index * per_ref + block) * stride
            out_ref[start : start + stride] = pay_ref[block]
            tile = pay_ref[block, rows:].astype(F32)
            ids.append((tile[0:1] * BASE + tile[1:2]).astype(jnp.int32))
    ids = jnp.concatenate(ids, axis=0)
    per_block = LANES // list_len
    queries = blocks * per_block
    block = lax.broadcasted_iota(jnp.int32, (blocks, LANES), 0)
    lane = lax.broadcasted_iota(jnp.int32, (blocks, LANES), 1)
    query = lane // list_len
    source = (block * stride + query * (rows // per_block)).astype(F32)
    quarter = blocks // 4
    region = block // quarter
    moved = block + jnp.where(region == 1, quarter, 0) - jnp.where(region == 2, quarter, 0)
    first = lane % list_len == 0
    target = jnp.where(first, queries + moved * per_block, block * per_block) + query
    target = (target - 2 * queries).astype(F32)
    upper = lax.broadcasted_iota(jnp.int32, (LANES, LANES), 0)
    column = lax.broadcasted_iota(jnp.int32, (LANES, LANES), 1)
    triangle = (upper <= column).astype(F32)
    diagonal = upper == column
    parts = list_ref.shape[2]
    place = lax.broadcasted_iota(jnp.int32, (parts * LANES, LANES), 0).astype(F32)
    for piece in range(list_ref.shape[0]):
        held = jnp.full((blocks, LANES), -1, jnp.int32)
        for index in range(size):
            held = jnp.where(ids == docs_ref[piece * size + index], index, held)
        mask = held >= 0
        code = held.astype(F32) * SHIFT + source
        ranks = jnp.dot(mask.astype(F32), triangle, preferred_element_type=F32)
        before = jnp.zeros((1, 1), F32)
        codes = jnp.zeros((parts * LANES, LANES), F32)
        targets = jnp.zeros((parts * LANES, LANES), F32)
        for index in range(blocks):
            row = ranks[index : index + 1]
            slot = jnp.where(mask[index : index + 1], before + row - 1.0, -1.0)
            here = place == slot
            codes = codes + jnp.where(here, code[index : index + 1], 0.0)
            targets = targets + jnp.where(here, target[index : index + 1], 0.0)
            before = before + row[:, LANES - 1 : LANES]
        for kind, found in enumerate((codes, targets + 2.0 * queries / LANES)):
            packed = jnp.sum(found, axis=1, keepdims=True)
            for part in range(parts):
                value = packed[part * LANES : (part + 1) * LANES]
                line = jnp.sum(jnp.where(diagonal, value, 0.0), axis=0, keepdims=True)
                list_ref[piece, kind, part : part + 1] = line.astype(jnp.int32)
        count = jnp.broadcast_to(before, (parts, LANES)).astype(jnp.int32)
        list_ref[piece, 2] = count


def score_pairs(list_ref, pay_ref, pass_ref, turned_ref, acc_ref, sums_ref, length):
    queries = sums_ref.shape[0] // 2
    count = list_ref[2, 0, 0]

    def step(index, carry):
        pairs = []
        for offset in range(UNROLL):
            slot = index * UNROLL + offset
            part, lane = lax.shift_right_logical(slot, 7), slot & (LANES - 1)
            code = list_ref[0, part, lane]
            row = pl.multiple_of(code & (SHIFT - 1), 16)
            place = lax.shift_right_logical(code, SHIFT.bit_length() - 1)
            pairs.append((list_ref[1, part, lane], pay_ref[pl.ds(row, length)], place))
        logits = [
            jnp.dot(tokens, turned_ref[place], preferred_element_type=F32)
            for _, tokens, place in pairs
        ]
        terms = [jnp.exp(block * (1.0 / SOFTNESS)) for block in logits]
        masses = [jnp.sum(block, axis=1, keepdims=True) for block in terms]
        pulled = [
            jnp.dot(block.astype(BF16), pass_ref[pair[2]], preferred_element_type=F32)
            for block, pair in zip(terms, pairs)
        ]
        done = []
        for (target, _, _), mass, rows in zip(pairs, masses, pulled):
            score = SOFTNESS * jnp.sum(jnp.log(mass), axis=0, keepdims=True)
            exp_score = jnp.exp(score)
            first = target >= queries
            factor = jnp.where(first, 1.0, exp_score)
            done.append((target, rows * (factor / mass), jnp.where(first, score, exp_score)))
        for target, product, value in done:
            at = pl.ds(pl.multiple_of(target * length, length), length)
            acc_ref[at] = acc_ref[at] + product
            sums_ref[pl.ds(target, 1)] = sums_ref[pl.ds(target, 1)] + value
        return carry

    lax.fori_loop(0, lax.div(count + UNROLL - 1, UNROLL), step, 0)


def near_score_body(lists_ref, pay_ref, *refs, length):
    *pass_refs, acc_ref, sums_ref, list_ref, sem = refs
    move = pltpu.make_async_copy(lists_ref.at[: len(pass_refs) // 2], list_ref, sem)
    move.start()
    acc_ref[...] = jnp.zeros_like(acc_ref)
    sums_ref[...] = jnp.zeros_like(sums_ref)
    move.wait()
    for piece in range(len(pass_refs) // 2):
        score_pairs(
            list_ref.at[piece],
            pay_ref,
            pass_refs[2 * piece],
            pass_refs[2 * piece + 1],
            acc_ref,
            sums_ref,
            length,
        )


def far_score_body(lists_ref, pay_ref, raw_ref, _, __, acc_ref, sums_ref, *refs, piece, length):
    *send_refs, pass_ref, turned_ref, list_ref, sem = refs
    move = pltpu.make_async_copy(lists_ref.at[piece], list_ref, sem)
    move.start()
    turn_units(raw_ref, pass_ref, turned_ref)
    move.wait()
    score_pairs(list_ref, pay_ref, pass_ref, turned_ref, acc_ref, sums_ref, length)
    if send_refs:
        others_ref, firsts_ref = send_refs
        half = others_ref.shape[0]
        others_ref[...] = acc_ref[half : 2 * half].astype(BF16)
        firsts_ref[...] = acc_ref[3 * half : 4 * half].astype(BF16)


def halve_body(acc_ref, others_ref, firsts_ref, send_a, send_b, keep_a, keep_b):
    half = others_ref.shape[0]
    quarter = half // 2
    for start, got, send, keep in (
        (0, others_ref, send_a, keep_a),
        (2 * half, firsts_ref, send_b, keep_b),
    ):
        keep[...] = acc_ref[start : start + quarter] + got[:quarter].astype(F32)
        rest = acc_ref[start + quarter : start + half] + got[quarter:].astype(F32)
        send[...] = rest.astype(BF16)


def merge_body(others_ref, got_others, firsts_ref, got_firsts, sums_ref, send_ref, rest_ref, *, length):
    queries = sums_ref.shape[1]

    def part(index):
        at = slice(index * length, (index + 1) * length)
        others = others_ref[at] + got_others[at].astype(F32)
        first = firsts_ref[at] + got_firsts[at].astype(F32)
        return others - sums_ref[0, index : index + 1] * first

    for index in range(queries // 2):
        at = slice(index * length, (index + 1) * length)
        rest_ref[at] = part(index)
        send_ref[at] = part(index + queries // 2).astype(BF16)


def last_body(queries_ref, keep_ref, got_ref, sums_ref, grad_ref, loss_ref, *, length):
    count = queries_ref.shape[0]
    losses = []
    for index in range(count):
        at = slice(index * length, (index + 1) * length)
        spread = sums_ref[0, index : index + 1]
        score = sums_ref[1, index : index + 1]
        total = spread + jnp.exp(score)
        losses.append(jnp.log(total) - score)
        gradient = (keep_ref[at] + got_ref[at].astype(F32)) / total
        query_unit, query_scale = unit(queries_ref[index])
        along = jnp.sum(query_unit * gradient, axis=-1, keepdims=True)
        grad_ref[index] = (gradient - query_unit * along) * query_scale
    losses = jnp.concatenate(losses, axis=0)
    place = lax.broadcasted_iota(jnp.int32, (count, LANES), 0)
    lane = lax.broadcasted_iota(jnp.int32, (count, LANES), 1)
    loss_ref[...] = jnp.sum(jnp.where(place == lane, losses, 0.0), axis=0, keepdims=True)[:, :count]


def swap(value, axis, bit):
    size = lax.axis_size(axis)
    return lax.ppermute(value, axis, [(index, index ^ bit) for index in range(size)])


def bits_of(size):
    return [1 << power for power in reversed(range(size.bit_length() - 1))]


def spread_offsets(size):
    offsets = [0]
    for bit in bits_of(size):
        offsets = offsets + [offset ^ bit for offset in offsets]
    return offsets


def spread(block):
    blocks = [block]
    for bit in bits_of(lax.axis_size("group") // 2):
        blocks = blocks + [swap(held, "group", bit) for held in blocks]
    return blocks


def local(queries, passages, candidates, location):
    group_count = lax.axis_size("group")
    dev_count = lax.axis_size("dev")
    device_total = group_count * dev_count
    query_count, length, width = queries.shape
    pass_count, pass_len, _ = passages.shape
    list_len = candidates.shape[1]
    pair_count = query_count * list_len
    rows = query_count * length
    slot_cap = max(2, (3 * pair_count + device_total - 1) // device_total)
    group = lax.axis_index("group")
    dev = lax.axis_index("dev")
    shape = jax.ShapeDtypeStruct

    half_bit = group_count // 2
    far_raw = swap(passages, "group", half_bit)
    near_raw = spread(passages)
    hbm, smem, vmem = (
        pl.BlockSpec(memory_space=space) for space in (pltpu.HBM, pltpu.SMEM, pltpu.VMEM)
    )
    payload = call(
        pack_body,
        shape((rows + TAIL, width), BF16),
        "query_units",
        [vmem, vmem],
    )(queries, candidates)

    *first_bits, low, lowest = bits_of(dev_count)
    pay = payload[None]
    for bit in first_bits:
        pay = jnp.concatenate([pay, swap(pay, "dev", bit)], axis=0)
    turned = shape((pass_count, width, pass_len), BF16)
    near = call(unit_body, [shape(passages.shape, BF16), turned] * len(near_raw), "passage_units")(
        *near_raw
    )
    pay_low = swap(pay, "dev", low)
    pays = [pay, pay_low, swap(pay, "dev", lowest), swap(pay_low, "dev", lowest)]
    pays[3], near = lax.optimization_barrier((pays[3], near))

    near_offsets = spread_offsets(half_bit)
    offsets = near_offsets + [offset ^ half_bit for offset in near_offsets]
    held_rows = jnp.concatenate(
        [
            ((group ^ offset) * dev_count + dev) * pass_count + jnp.arange(pass_count)
            for offset in offsets
        ]
    )
    hits = location[None, :] == held_rows.astype(jnp.int32)[:, None]
    documents = jnp.arange(location.shape[0], dtype=jnp.int32)
    docs = jnp.sum(jnp.where(hits, documents[None, :], 0), axis=1)

    parts = -(-dev_count * min(pair_count, slot_cap) // LANES)
    pay, lists = call(
        functools.partial(route_body, rows=rows, size=pass_count, list_len=list_len),
        [
            shape((dev_count * (rows + TAIL), width), BF16),
            shape((len(offsets), 3, parts, LANES), jnp.int32),
        ],
        "route",
        in_specs=[smem] + [vmem] * len(pays),
    )(docs, *pays)

    all_queries = dev_count * query_count
    half_rows = all_queries * length // 2
    totals = [
        shape(((2 * all_queries + 1) * length, width), F32),
        shape((2 * all_queries + 1, LANES), F32),
    ]
    sends = [shape((half_rows, width), BF16)] * 2
    state = call(
        functools.partial(near_score_body, length=length),
        totals,
        "score_near",
        [vmem] * (2 + len(near)),
        scratch=[
            pltpu.SMEM((len(near_raw), 3, parts, LANES), jnp.int32),
            pltpu.SemaphoreType.DMA(()),
        ],
    )(lists, pay, *near)
    far_raw, *state = lax.optimization_barrier((far_raw, *state))
    far = spread(far_raw)
    for index, raw in enumerate(far):
        last = index == len(far) - 1
        state = call(
            functools.partial(far_score_body, piece=len(far) + index, length=length),
            totals + (sends if last else []),
            "score_far",
            [vmem] * 5,
            {3: 0, 4: 1},
            [
                pltpu.VMEM(passages.shape, BF16),
                pltpu.VMEM(turned.shape, BF16),
                pltpu.SMEM((3, parts, LANES), jnp.int32),
                pltpu.SemaphoreType.DMA(()),
            ],
        )(lists, pay, raw, *state)
    acc, sums, others, firsts = state

    steps = bits_of(dev_count)[::-1]
    got_others = swap(others, "dev", steps[0])
    got_firsts = swap(firsts, "dev", steps[1])
    sums = sums[: 2 * all_queries].reshape(2, 2, 2, all_queries // 4, LANES)
    spreads, scores = sums[0], jnp.swapaxes(sums[1], 0, 1)
    sums = jnp.stack([spreads[0], scores[0]])
    sums = sums + swap(jnp.stack([spreads[1], scores[1]]), "dev", steps[0])
    levels = len(steps) - 2
    halves = [sums[:, index].reshape((2,) + (2,) * levels + (query_count, LANES)) for index in (0, 1)]
    sums = halves[0]
    for mask in range(1, 2 << levels):
        turned_halves = halves[mask & 1]
        axes = [1 + level for level in range(levels) if mask >> (level + 1) & 1]
        bits = sum(bit for place, bit in enumerate(steps[1:]) if mask >> place & 1)
        sums = sums + swap(jnp.flip(turned_halves, axis=axes), "dev", bits)
    sums = sums.reshape(2, all_queries // 4, LANES)
    quarter = half_rows // 2
    send_others, send_firsts, others, firsts = call(
        halve_body, [shape((quarter, width), BF16)] * 2 + [shape((quarter, width), F32)] * 2, "halve"
    )(acc, got_others, got_firsts)
    got_others = swap(send_others, "dev", steps[1])
    got_firsts = swap(send_firsts, "dev", steps[0])
    quarter = quarter // 2
    send, rest = call(
        functools.partial(merge_body, length=length),
        [shape((quarter, width), BF16), shape((quarter, width), F32)],
        "merge",
    )(others, got_others, firsts, got_firsts, sums)
    for bit in steps[2:-1]:
        rest = rest + swap(send, "dev", bit).astype(F32)
        quarter = quarter // 2
        rest, send = rest[:quarter], rest[quarter:].astype(BF16)
    got = swap(send, "dev", steps[-1])
    grad, loss = call(
        functools.partial(last_body, length=length),
        [shape(queries.shape, F32), shape((1, query_count), F32)],
        "last",
    )(queries, rest, got, sums[:, :query_count])
    return loss.reshape(query_count), grad


def solution(mesh):
    placed = (
        P(("group", "dev"), None, None),
        P(("group", "dev"), None, None),
        P(("group", "dev"), None),
        P(),
    )
    return jax.shard_map(
        local,
        mesh=mesh,
        in_specs=placed,
        out_specs=(P(("group", "dev")), P(("group", "dev"), None, None)),
        check_vma=False,
    )
```

```python
import functools

import jax
import jax.numpy as jnp
from jax import lax
from jax.experimental import pallas as pl
from jax.experimental.pallas import tpu as pltpu
from jax.sharding import PartitionSpec as P

SOFTNESS = 0.02
EPSILON = 1e-06
LANES = 128
TAIL = 16
BASE = 256
UNROLL = 16
SHIFT = 1 << 16
F32 = jnp.float32
BF16 = jnp.bfloat16


def call(body, out_shape, name, in_specs=None, aliases={}, scratch=(), cost=0):
    kwargs = {} if in_specs is None else {"in_specs": in_specs}
    return pl.pallas_call(
        body,
        out_shape=out_shape,
        input_output_aliases=aliases,
        scratch_shapes=list(scratch),
        name=name,
        cost_estimate=pl.CostEstimate(flops=0, bytes_accessed=cost, transcendentals=0),
        compiler_params=pltpu.CompilerParams(vmem_limit_bytes=20 * 1024 * 1024),
        **kwargs,
    )


def unit(values):
    floats = values.astype(F32)
    scale = lax.rsqrt(jnp.sum(floats * floats, axis=-1, keepdims=True) + EPSILON)
    return floats * scale, scale


def pack_body(queries_ref, cand_ref, out_ref):
    count, length, width = queries_ref.shape
    rows = count * length
    out_ref[:rows] = unit(queries_ref[...])[0].astype(BF16).reshape(rows, width)
    ids = jnp.concatenate([cand_ref[index : index + 1] for index in range(count)], axis=1)
    ids = jnp.broadcast_to(ids, (TAIL, LANES))
    high = ids // BASE
    low = ids - high * BASE
    place = lax.broadcasted_iota(jnp.int32, (TAIL, LANES), 0)
    digits = jnp.where(place == 0, high, jnp.where(place == 1, low, 0))
    out_ref[rows:] = digits.astype(F32).astype(BF16)


def turn_units(source, units_ref, turned_ref):
    count = source.shape[0]
    together = min(count, 8)

    def step(index, carry):
        for offset in range(together):
            at = index * together + offset
            units = unit(source[at])[0].astype(BF16)
            units_ref[at] = units
            turned_ref[at] = units.T
        return carry

    lax.fori_loop(0, count // together, step, 0)


def unit_body(*refs):
    half = len(refs) // 3
    for index, source in enumerate(refs[:half]):
        turn_units(source, refs[half + 2 * index], refs[half + 2 * index + 1])


def route_body(docs_ref, *refs, rows, size, groups_of, list_len):
    *pay_refs, out_ref, list_ref = refs
    per_ref = pay_refs[0].shape[0]
    blocks = per_ref * len(pay_refs)
    stride = rows + TAIL
    ids = []
    for index, pay_ref in enumerate(pay_refs):
        for block in range(per_ref):
            start = (index * per_ref + block) * stride
            out_ref[start : start + stride] = pay_ref[block]
            tile = pay_ref[block, rows:].astype(F32)
            ids.append((tile[0:1] * BASE + tile[1:2]).astype(jnp.int32))
    ids = jnp.concatenate(ids, axis=0)
    per_block = LANES // list_len
    queries = blocks * per_block
    block = lax.broadcasted_iota(jnp.int32, (blocks, LANES), 0)
    lane = lax.broadcasted_iota(jnp.int32, (blocks, LANES), 1)
    query = lane // list_len
    source = (block * stride + query * (rows // per_block)).astype(F32)
    quarter = blocks // 4
    region = block // quarter
    moved = block + jnp.where(region == 1, quarter, 0) - jnp.where(region == 2, quarter, 0)
    first = lane % list_len == 0
    target = jnp.where(first, queries + moved * per_block, block * per_block) + query
    target = (target - 2 * queries).astype(F32)
    upper = lax.broadcasted_iota(jnp.int32, (LANES, LANES), 0)
    column = lax.broadcasted_iota(jnp.int32, (LANES, LANES), 1)
    triangle = (upper <= column).astype(F32)
    diagonal = upper == column
    parts = list_ref.shape[2]
    place = lax.broadcasted_iota(jnp.int32, (parts * LANES, LANES), 0).astype(F32)
    leaving = (block >= 2 * quarter) | (first & (region == 1))
    for index, groups in enumerate(groups_of):
        held = jnp.full((blocks, LANES), -1, jnp.int32)
        for place_of in range(size):
            held = jnp.where(ids == docs_ref[index * size + place_of], place_of, held)
        code = held.astype(F32) * SHIFT + source
        for piece, group in groups:
            mask = held >= 0
            if group is not None:
                mask = mask & (leaving if group == 0 else jnp.logical_not(leaving))
            ranks = jnp.dot(mask.astype(F32), triangle, preferred_element_type=F32)
            before = jnp.zeros((1, 1), F32)
            codes = jnp.zeros((parts * LANES, LANES), F32)
            targets = jnp.zeros((parts * LANES, LANES), F32)
            for row_of in range(blocks):
                row = ranks[row_of : row_of + 1]
                slot = jnp.where(mask[row_of : row_of + 1], before + row - 1.0, -1.0)
                here = place == slot
                codes = codes + jnp.where(here, code[row_of : row_of + 1], 0.0)
                targets = targets + jnp.where(here, target[row_of : row_of + 1], 0.0)
                before = before + row[:, LANES - 1 : LANES]
            for kind, found in enumerate((codes, targets + 2.0 * queries / LANES)):
                packed = jnp.sum(found, axis=1, keepdims=True)
                for part in range(parts):
                    value = packed[part * LANES : (part + 1) * LANES]
                    line = jnp.sum(jnp.where(diagonal, value, 0.0), axis=0, keepdims=True)
                    list_ref[piece, kind, part : part + 1] = line.astype(jnp.int32)
            list_ref[piece, 2] = jnp.broadcast_to(before, (parts, LANES)).astype(jnp.int32)


def score_pairs(list_ref, pay_ref, pass_ref, turned_ref, acc_ref, sums_ref, length):
    queries = sums_ref.shape[0] // 2
    count = list_ref[2, 0, 0]

    def step(index, carry):
        pairs = []
        for offset in range(UNROLL):
            slot = index * UNROLL + offset
            part, lane = lax.shift_right_logical(slot, 7), slot & (LANES - 1)
            code = list_ref[0, part, lane]
            row = pl.multiple_of(code & (SHIFT - 1), 16)
            place = lax.shift_right_logical(code, SHIFT.bit_length() - 1)
            pairs.append((list_ref[1, part, lane], pay_ref[pl.ds(row, length)], place))
        logits = [
            jnp.dot(tokens, turned_ref[place], preferred_element_type=F32)
            for _, tokens, place in pairs
        ]
        terms = [jnp.exp(block * (1.0 / SOFTNESS)) for block in logits]
        masses = [jnp.sum(block, axis=1, keepdims=True) for block in terms]
        pulled = [
            jnp.dot(block.astype(BF16), pass_ref[pair[2]], preferred_element_type=F32)
            for block, pair in zip(terms, pairs)
        ]
        done = []
        for (target, _, _), mass, rows in zip(pairs, masses, pulled):
            score = SOFTNESS * jnp.sum(jnp.log(mass), axis=0, keepdims=True)
            exp_score = jnp.exp(score)
            first = target >= queries
            factor = jnp.where(first, 1.0, exp_score)
            done.append((target, rows * (factor / mass), jnp.where(first, score, exp_score)))
        for target, product, value in done:
            at = pl.ds(pl.multiple_of(target * length, length), length)
            acc_ref[at] = acc_ref[at] + product
            sums_ref[pl.ds(target, 1)] = sums_ref[pl.ds(target, 1)] + value
        return carry

    lax.fori_loop(0, lax.div(count + UNROLL - 1, UNROLL), step, 0)


def score_body(lists_ref, pay_ref, *refs, piece, count, begin, length):
    pass_refs, refs = refs[: 2 * count], refs[2 * count :]
    acc_ref, sums_ref, list_ref, sem = refs if begin else refs[2:]
    move = pltpu.make_async_copy(lists_ref.at[piece : piece + count], list_ref, sem)
    move.start()
    if begin:
        acc_ref[...] = jnp.zeros_like(acc_ref)
        sums_ref[...] = jnp.zeros_like(sums_ref)
    move.wait()
    for index in range(count):
        score_pairs(
            list_ref.at[index],
            pay_ref,
            pass_refs[2 * index],
            pass_refs[2 * index + 1],
            acc_ref,
            sums_ref,
            length,
        )


def far_score_body(
    lists_ref, pay_ref, raw_ref, _, __, acc_ref, sums_ref, pass_ref, turned_ref, *refs, piece, length
):
    *send_refs, list_ref, sem = refs
    move = pltpu.make_async_copy(lists_ref.at[piece], list_ref, sem)
    move.start()
    turn_units(raw_ref, pass_ref, turned_ref)
    move.wait()
    score_pairs(list_ref, pay_ref, pass_ref, turned_ref, acc_ref, sums_ref, length)
    if send_refs:
        others_ref, firsts_ref = send_refs
        half = others_ref.shape[0]
        others_ref[...] = acc_ref[half : 2 * half].astype(BF16)
        firsts_ref[...] = acc_ref[3 * half : 4 * half].astype(BF16)


def halve_body(acc_ref, others_ref, firsts_ref, send_a, send_b, keep_a, keep_b):
    half = others_ref.shape[0]
    quarter = half // 2
    for start, got, send, keep in (
        (0, others_ref, send_a, keep_a),
        (2 * half, firsts_ref, send_b, keep_b),
    ):
        keep[...] = acc_ref[start : start + quarter] + got[:quarter].astype(F32)
        rest = acc_ref[start + quarter : start + half] + got[quarter:].astype(F32)
        send[...] = rest.astype(BF16)


def merge_body(others_ref, got_others, firsts_ref, got_firsts, sums_ref, send_ref, rest_ref, *, length):
    queries = sums_ref.shape[1]

    def part(index):
        at = slice(index * length, (index + 1) * length)
        others = others_ref[at] + got_others[at].astype(F32)
        first = firsts_ref[at] + got_firsts[at].astype(F32)
        return others - sums_ref[0, index : index + 1] * first

    for index in range(queries // 2):
        at = slice(index * length, (index + 1) * length)
        rest_ref[at] = part(index)
        send_ref[at] = part(index + queries // 2).astype(BF16)


def last_body(queries_ref, keep_ref, got_ref, sums_ref, grad_ref, loss_ref, *, length):
    count = queries_ref.shape[0]
    losses = []
    for index in range(count):
        at = slice(index * length, (index + 1) * length)
        spread = sums_ref[0, index : index + 1]
        score = sums_ref[1, index : index + 1]
        total = spread + jnp.exp(score)
        losses.append(jnp.log(total) - score)
        gradient = (keep_ref[at] + got_ref[at].astype(F32)) / total
        query_unit, query_scale = unit(queries_ref[index])
        along = jnp.sum(query_unit * gradient, axis=-1, keepdims=True)
        grad_ref[index] = (gradient - query_unit * along) * query_scale
    losses = jnp.concatenate(losses, axis=0)
    place = lax.broadcasted_iota(jnp.int32, (count, LANES), 0)
    lane = lax.broadcasted_iota(jnp.int32, (count, LANES), 1)
    loss_ref[...] = jnp.sum(jnp.where(place == lane, losses, 0.0), axis=0, keepdims=True)[:, :count]


def swap(value, axis, bit):
    size = lax.axis_size(axis)
    return lax.ppermute(value, axis, [(index, index ^ bit) for index in range(size)])


def bits_of(size):
    return [1 << power for power in reversed(range(size.bit_length() - 1))]


def spread_offsets(size):
    offsets = [0]
    for bit in bits_of(size):
        offsets = offsets + [offset ^ bit for offset in offsets]
    return offsets


def spread(block):
    blocks = [block]
    for bit in bits_of(lax.axis_size("group") // 2):
        blocks = blocks + [swap(held, "group", bit) for held in blocks]
    return blocks


def local(queries, passages, candidates, location):
    group_count = lax.axis_size("group")
    dev_count = lax.axis_size("dev")
    device_total = group_count * dev_count
    query_count, length, width = queries.shape
    pass_count, pass_len, _ = passages.shape
    list_len = candidates.shape[1]
    pair_count = query_count * list_len
    rows = query_count * length
    slot_cap = max(2, (3 * pair_count + device_total - 1) // device_total)
    group = lax.axis_index("group")
    dev = lax.axis_index("dev")
    shape = jax.ShapeDtypeStruct

    half_bit = group_count // 2
    far_raw = swap(passages, "group", half_bit)
    near_raw = spread(passages)
    hbm, smem, vmem = (
        pl.BlockSpec(memory_space=space) for space in (pltpu.HBM, pltpu.SMEM, pltpu.VMEM)
    )
    payload = call(
        pack_body,
        shape((rows + TAIL, width), BF16),
        "query_units",
        [vmem, vmem],
    )(queries, candidates)

    *first_bits, low, lowest = bits_of(dev_count)
    pay = payload[None]
    for bit in first_bits:
        pay = jnp.concatenate([pay, swap(pay, "dev", bit)], axis=0)
    turned = shape((pass_count, width, pass_len), BF16)
    near = call(unit_body, [shape(passages.shape, BF16), turned] * len(near_raw), "passage_units")(
        *near_raw
    )
    pay_low = swap(pay, "dev", low)
    pays = [pay, pay_low, swap(pay, "dev", lowest), swap(pay_low, "dev", lowest)]
    pays[3], near = lax.optimization_barrier((pays[3], near))

    near_offsets = spread_offsets(half_bit)
    offsets = near_offsets + [offset ^ half_bit for offset in near_offsets]
    held_rows = jnp.concatenate(
        [
            ((group ^ offset) * dev_count + dev) * pass_count + jnp.arange(pass_count)
            for offset in offsets
        ]
    )
    hits = location[None, :] == held_rows.astype(jnp.int32)[:, None]
    documents = jnp.arange(location.shape[0], dtype=jnp.int32)
    docs = jnp.sum(jnp.where(hits, documents[None, :], 0), axis=1)

    parts = -(-dev_count * min(pair_count, slot_cap) // LANES)
    near_count = len(near_offsets)
    groups_of = [((index, None),) for index in range(near_count)]
    groups_of += [((near_count + i, 0), (2 * near_count + i, 1)) for i in range(near_count)]
    pay, lists = call(
        functools.partial(
            route_body, rows=rows, size=pass_count, groups_of=groups_of, list_len=list_len
        ),
        [
            shape((dev_count * (rows + TAIL), width), BF16),
            shape((3 * near_count, 3, parts, LANES), jnp.int32),
        ],
        "route",
        in_specs=[smem] + [vmem] * len(pays),
    )(docs, *pays)

    all_queries = dev_count * query_count
    half_rows = all_queries * length // 2
    totals = [
        shape(((2 * all_queries + 1) * length, width), F32),
        shape((2 * all_queries + 1, LANES), F32),
    ]
    sends = [shape((half_rows, width), BF16)] * 2
    def score(blocks, piece, state=()):
        return call(
            functools.partial(
                score_body, piece=piece, count=near_count, begin=not state, length=length
            ),
            totals,
            "score",
            [vmem] * (2 + len(blocks) + len(state)),
            {2 + len(blocks): 0, 3 + len(blocks): 1} if state else {},
            [
                pltpu.SMEM((near_count, 3, parts, LANES), jnp.int32),
                pltpu.SemaphoreType.DMA(()),
            ],
        )(lists, pay, *blocks, *state)

    state = score(near, 0)
    far_raw, *state = lax.optimization_barrier((far_raw, *state))
    far = []
    for index, raw in enumerate(spread(far_raw)):
        last = index == near_count - 1
        acc, sums, *blocks = call(
            functools.partial(far_score_body, piece=near_count + index, length=length),
            totals + [shape(passages.shape, BF16), turned] + (sends if last else []),
            "score_far",
            [vmem] * 5,
            {3: 0, 4: 1},
            [pltpu.SMEM((3, parts, LANES), jnp.int32), pltpu.SemaphoreType.DMA(())],
        )(lists, pay, raw, *state)
        state = (acc, sums)
        far += blocks[:2]
    others, firsts = blocks[2:]

    steps = bits_of(dev_count)[::-1]
    got_others = swap(others, "dev", steps[0])
    got_firsts = swap(firsts, "dev", steps[1])
    def quarters(sums):
        spreads, scores = sums[: 2 * all_queries].reshape(2, 2, 2, all_queries // 4, LANES)
        return [jnp.stack([spreads[half], scores[:, half]]) for half in (0, 1)]

    got_sums = swap(quarters(sums)[1], "dev", steps[0])
    got_sums, *state = lax.optimization_barrier((got_sums, *state))
    acc, sums = score(far, 2 * near_count, state)
    sums = quarters(sums)[0] + got_sums
    levels = len(steps) - 2
    halves = [sums[:, index].reshape((2,) + (2,) * levels + (query_count, LANES)) for index in (0, 1)]
    sums = halves[0]
    for mask in range(1, 2 << levels):
        turned_halves = halves[mask & 1]
        axes = [1 + level for level in range(levels) if mask >> (level + 1) & 1]
        bits = sum(bit for place, bit in enumerate(steps[1:]) if mask >> place & 1)
        sums = sums + swap(jnp.flip(turned_halves, axis=axes), "dev", bits)
    sums = sums.reshape(2, all_queries // 4, LANES)
    quarter = half_rows // 2
    send_others, send_firsts, others, firsts = call(
        halve_body, [shape((quarter, width), BF16)] * 2 + [shape((quarter, width), F32)] * 2, "halve"
    )(acc, got_others, got_firsts)
    got_others = swap(send_others, "dev", steps[1])
    got_firsts = swap(send_firsts, "dev", steps[0])
    quarter = quarter // 2
    send, rest = call(
        functools.partial(merge_body, length=length),
        [shape((quarter, width), BF16), shape((quarter, width), F32)],
        "merge",
    )(others, got_others, firsts, got_firsts, sums)
    for bit in steps[2:-1]:
        rest = rest + swap(send, "dev", bit).astype(F32)
        quarter = quarter // 2
        rest, send = rest[:quarter], rest[quarter:].astype(BF16)
    got = swap(send, "dev", steps[-1])
    grad, loss = call(
        functools.partial(last_body, length=length),
        [shape(queries.shape, F32), shape((1, query_count), F32)],
        "last",
    )(queries, rest, got, sums[:, :query_count])
    return loss.reshape(query_count), grad


def solution(mesh):
    placed = (
        P(("group", "dev"), None, None),
        P(("group", "dev"), None, None),
        P(("group", "dev"), None),
        P(),
    )
    return jax.shard_map(
        local,
        mesh=mesh,
        in_specs=placed,
        out_specs=(P(("group", "dev")), P(("group", "dev"), None, None)),
        check_vma=False,
    )
```

```python
import functools

import jax
import jax.numpy as jnp
from jax import lax
from jax.experimental import pallas as pl
from jax.experimental.pallas import tpu as pltpu
from jax.sharding import PartitionSpec as P

SOFTNESS = 0.02
EPSILON = 1e-06
LANES = 128
TAIL = 16
BASE = 256
UNROLL = 20
SHIFT = 1 << 16
F32 = jnp.float32
BF16 = jnp.bfloat16


def call(body, out_shape, name, in_specs=None, aliases={}, scratch=()):
    kwargs = {} if in_specs is None else {"in_specs": in_specs}
    return pl.pallas_call(
        body,
        out_shape=out_shape,
        input_output_aliases=aliases,
        scratch_shapes=list(scratch),
        name=name,
        cost_estimate=pl.CostEstimate(flops=0, bytes_accessed=0, transcendentals=0),
        compiler_params=pltpu.CompilerParams(vmem_limit_bytes=20 * 1024 * 1024),
        **kwargs,
    )


def unit(values):
    floats = values.astype(F32)
    scale = lax.rsqrt(jnp.sum(floats * floats, axis=-1, keepdims=True) + EPSILON)
    return floats * scale, scale


def pack_body(queries_ref, cand_ref, out_ref):
    count, length, width = queries_ref.shape
    rows = count * length
    out_ref[:rows] = unit(queries_ref[...])[0].astype(BF16).reshape(rows, width)
    ids = jnp.concatenate([cand_ref[index : index + 1] for index in range(count)], axis=1)
    ids = jnp.broadcast_to(ids, (TAIL, LANES))
    high = ids // BASE
    low = ids - high * BASE
    place = lax.broadcasted_iota(jnp.int32, (TAIL, LANES), 0)
    digits = jnp.where(place == 0, high, jnp.where(place == 1, low, 0))
    out_ref[rows:] = digits.astype(F32).astype(BF16)


def turn_units(source, units_ref, turned_ref):
    count = source.shape[0]
    together = min(count, 16)

    def step(index, carry):
        for offset in range(together):
            at = index * together + offset
            units = unit(source[at])[0].astype(BF16)
            units_ref[at] = units
            turned_ref[at] = units.T
        return carry

    lax.fori_loop(0, count // together, step, 0)


def unit_body(*refs):
    half = len(refs) // 3
    for index, source in enumerate(refs[:half]):
        turn_units(source, refs[half + 2 * index], refs[half + 2 * index + 1])


def route_body(docs_ref, *refs, rows, size, groups_of, list_len):
    *pay_refs, out_ref, list_ref = refs
    per_ref = pay_refs[0].shape[0]
    blocks = per_ref * len(pay_refs)
    stride = rows + TAIL
    ids = []
    for index, pay_ref in enumerate(pay_refs):
        for block in range(per_ref):
            start = (index * per_ref + block) * stride
            out_ref[start : start + stride] = pay_ref[block]
            tile = pay_ref[block, rows:].astype(F32)
            ids.append((tile[0:1] * BASE + tile[1:2]).astype(jnp.int32))
    ids = jnp.concatenate(ids, axis=0)
    per_block = LANES // list_len
    queries = blocks * per_block
    block = lax.broadcasted_iota(jnp.int32, (blocks, LANES), 0)
    lane = lax.broadcasted_iota(jnp.int32, (blocks, LANES), 1)
    query = lane // list_len
    source = (block * stride + query * (rows // per_block)).astype(F32)
    quarter = blocks // 4
    region = block // quarter
    moved = block + jnp.where(region == 1, quarter, 0) - jnp.where(region == 2, quarter, 0)
    first = lane % list_len == 0
    target = jnp.where(first, queries + moved * per_block, block * per_block) + query
    target = (target - 2 * queries).astype(F32)
    upper = lax.broadcasted_iota(jnp.int32, (LANES, LANES), 0)
    column = lax.broadcasted_iota(jnp.int32, (LANES, LANES), 1)
    triangle = (upper <= column).astype(F32)
    diagonal = upper == column
    parts = list_ref.shape[2]
    place = lax.broadcasted_iota(jnp.int32, (parts * LANES, LANES), 0).astype(F32)
    leaving = (block >= 2 * quarter) | (first & (region == 1))
    for index, groups in enumerate(groups_of):
        held = jnp.full((blocks, LANES), -1, jnp.int32)
        for place_of in range(size):
            held = jnp.where(ids == docs_ref[index * size + place_of], place_of, held)
        code = held.astype(F32) * SHIFT + source
        for piece, group in groups:
            mask = held >= 0
            if group is not None:
                mask = mask & (leaving if group == 0 else jnp.logical_not(leaving))
            ranks = jnp.dot(mask.astype(F32), triangle, preferred_element_type=F32)
            before = jnp.zeros((1, 1), F32)
            codes = jnp.zeros((parts * LANES, LANES), F32)
            targets = jnp.zeros((parts * LANES, LANES), F32)
            for row_of in range(blocks):
                row = ranks[row_of : row_of + 1]
                slot = jnp.where(mask[row_of : row_of + 1], before + row - 1.0, -1.0)
                here = place == slot
                codes = codes + jnp.where(here, code[row_of : row_of + 1], 0.0)
                targets = targets + jnp.where(here, target[row_of : row_of + 1], 0.0)
                before = before + row[:, LANES - 1 : LANES]
            for kind, found in enumerate((codes, targets + 2.0 * queries / LANES)):
                packed = jnp.sum(found, axis=1, keepdims=True)
                for part in range(parts):
                    value = packed[part * LANES : (part + 1) * LANES]
                    line = jnp.sum(jnp.where(diagonal, value, 0.0), axis=0, keepdims=True)
                    list_ref[piece, kind, part : part + 1] = line.astype(jnp.int32)
            list_ref[piece, 2] = jnp.broadcast_to(before, (parts, LANES)).astype(jnp.int32)


def score_pairs(list_ref, pay_ref, pass_ref, turned_ref, acc_ref, sums_ref, length):
    queries = sums_ref.shape[0] // 2
    count = list_ref[2, 0, 0]

    def step(index, carry):
        pairs = []
        for offset in range(UNROLL):
            slot = index * UNROLL + offset
            part, lane = lax.shift_right_logical(slot, 7), slot & (LANES - 1)
            code = list_ref[0, part, lane]
            row = pl.multiple_of(code & (SHIFT - 1), 16)
            place = lax.shift_right_logical(code, SHIFT.bit_length() - 1)
            pairs.append((list_ref[1, part, lane], pay_ref[pl.ds(row, length)], place))
        logits = [
            jnp.dot(tokens, turned_ref[place], preferred_element_type=F32)
            for _, tokens, place in pairs
        ]
        terms = [jnp.exp(block * (1.0 / SOFTNESS)) for block in logits]
        masses = [jnp.sum(block, axis=1, keepdims=True) for block in terms]
        pulled = [
            jnp.dot(block.astype(BF16), pass_ref[pair[2]], preferred_element_type=F32)
            for block, pair in zip(terms, pairs)
        ]
        done = []
        for (target, _, _), mass, rows in zip(pairs, masses, pulled):
            score = SOFTNESS * jnp.sum(jnp.log(mass), axis=0, keepdims=True)
            exp_score = jnp.exp(score)
            first = target >= queries
            factor = jnp.where(first, 1.0, exp_score)
            done.append((target, rows * (factor / mass), jnp.where(first, score, exp_score)))
        for target, product, value in done:
            at = pl.ds(pl.multiple_of(target * length, length), length)
            acc_ref[at] = acc_ref[at] + product
            sums_ref[pl.ds(target, 1)] = sums_ref[pl.ds(target, 1)] + value
        return carry

    lax.fori_loop(0, lax.div(count + UNROLL - 1, UNROLL), step, 0)


def score_body(lists_ref, pay_ref, *refs, piece, count, begin, length):
    pass_refs, refs = refs[: 2 * count], refs[2 * count :]
    acc_ref, sums_ref, list_ref, sem = refs if begin else refs[2:]
    move = pltpu.make_async_copy(lists_ref.at[piece : piece + count], list_ref, sem)
    move.start()
    if begin:
        acc_ref[...] = jnp.zeros_like(acc_ref)
        sums_ref[...] = jnp.zeros_like(sums_ref)
    move.wait()
    for index in range(count):
        score_pairs(
            list_ref.at[index],
            pay_ref,
            pass_refs[2 * index],
            pass_refs[2 * index + 1],
            acc_ref,
            sums_ref,
            length,
        )


def far_score_body(
    lists_ref, pay_ref, raw_ref, _, __, acc_ref, sums_ref, pass_ref, turned_ref, *refs, piece, length
):
    *send_refs, list_ref, sem = refs
    move = pltpu.make_async_copy(lists_ref.at[piece], list_ref, sem)
    move.start()
    turn_units(raw_ref, pass_ref, turned_ref)
    move.wait()
    score_pairs(list_ref, pay_ref, pass_ref, turned_ref, acc_ref, sums_ref, length)
    if send_refs:
        others_ref, firsts_ref = send_refs
        half = others_ref.shape[0]
        others_ref[...] = acc_ref[half : 2 * half].astype(BF16)
        firsts_ref[...] = acc_ref[3 * half : 4 * half].astype(BF16)


def halve_body(acc_ref, got_others, got_firsts, *send_refs):
    for index, send_ref in enumerate(send_refs):
        got, region = ((got_others, 1), (got_firsts, 5))[index % 2]
        size = send_ref.shape[0]
        at = (1 - index // 2) * size
        own = acc_ref[region * 2 * size + at : region * 2 * size + at + size]
        rest = got[2 * size + at : 2 * size + at + size].astype(F32)
        send_ref[...] = (own + rest).astype(BF16)


def merge_body(acc_ref, others_ref, firsts_ref, got_others, got_firsts, sums_ref, out_ref, *, part, length):
    rows = out_ref.shape[0]
    for index in range(rows // length):
        at = slice(index * length, (index + 1) * length)
        here = slice(part * rows + index * length, part * rows + (index + 1) * length)
        behind = slice(8 * rows + here.start, 8 * rows + here.stop)
        others = acc_ref[here] + others_ref[here].astype(F32) + got_others[at].astype(F32)
        first = acc_ref[behind] + firsts_ref[here].astype(F32) + got_firsts[at].astype(F32)
        query = part * (rows // length) + index
        out_ref[at] = (others - sums_ref[0, query : query + 1] * first).astype(out_ref.dtype)


def last_body(queries_ref, keep_ref, got_ref, sums_ref, grad_ref, loss_ref, *, length):
    count = queries_ref.shape[0]
    losses = []
    for index in range(count):
        at = slice(index * length, (index + 1) * length)
        spread = sums_ref[0, index : index + 1]
        score = sums_ref[1, index : index + 1]
        total = spread + jnp.exp(score)
        losses.append(jnp.log(total) - score)
        gradient = (keep_ref[at] + got_ref[at].astype(F32)) / total
        query_unit, query_scale = unit(queries_ref[index])
        along = jnp.sum(query_unit * gradient, axis=-1, keepdims=True)
        grad_ref[index] = (gradient - query_unit * along) * query_scale
    losses = jnp.concatenate(losses, axis=0)
    place = lax.broadcasted_iota(jnp.int32, (count, LANES), 0)
    lane = lax.broadcasted_iota(jnp.int32, (count, LANES), 1)
    loss_ref[...] = jnp.sum(jnp.where(place == lane, losses, 0.0), axis=0, keepdims=True)[:, :count]


def swap(value, axis, bit):
    size = lax.axis_size(axis)
    return lax.ppermute(value, axis, [(index, index ^ bit) for index in range(size)])


def bits_of(size):
    return [1 << power for power in reversed(range(size.bit_length() - 1))]


def spread_offsets(size):
    offsets = [0]
    for bit in bits_of(size):
        offsets = offsets + [offset ^ bit for offset in offsets]
    return offsets


def spread(block):
    blocks = [block]
    for bit in bits_of(lax.axis_size("group") // 2):
        blocks = blocks + [swap(held, "group", bit) for held in blocks]
    return blocks


def local(queries, passages, candidates, location):
    group_count = lax.axis_size("group")
    dev_count = lax.axis_size("dev")
    device_total = group_count * dev_count
    query_count, length, width = queries.shape
    pass_count, pass_len, _ = passages.shape
    list_len = candidates.shape[1]
    pair_count = query_count * list_len
    rows = query_count * length
    slot_cap = max(2, (3 * pair_count + device_total - 1) // device_total)
    group = lax.axis_index("group")
    dev = lax.axis_index("dev")
    shape = jax.ShapeDtypeStruct

    half_bit = group_count // 2
    far_raw = swap(passages, "group", half_bit)
    near_raw = spread(passages)
    hbm, smem, vmem = (
        pl.BlockSpec(memory_space=space) for space in (pltpu.HBM, pltpu.SMEM, pltpu.VMEM)
    )
    payload = call(
        pack_body,
        shape((rows + TAIL, width), BF16),
        "query_units",
        [vmem, vmem],
    )(queries, candidates)

    *first_bits, low, lowest = bits_of(dev_count)
    pay = payload[None]
    for bit in first_bits:
        pay = jnp.concatenate([pay, swap(pay, "dev", bit)], axis=0)
    turned = shape((pass_count, width, pass_len), BF16)
    near = call(unit_body, [shape(passages.shape, BF16), turned] * len(near_raw), "passage_units")(
        *near_raw
    )
    pay_low = swap(pay, "dev", low)
    pays = [pay, pay_low, swap(pay, "dev", lowest), swap(pay_low, "dev", lowest)]
    pays[3], near = lax.optimization_barrier((pays[3], near))

    near_offsets = spread_offsets(half_bit)
    offsets = near_offsets + [offset ^ half_bit for offset in near_offsets]
    held_rows = jnp.concatenate(
        [
            ((group ^ offset) * dev_count + dev) * pass_count + jnp.arange(pass_count)
            for offset in offsets
        ]
    )
    hits = location[None, :] == held_rows.astype(jnp.int32)[:, None]
    documents = jnp.arange(location.shape[0], dtype=jnp.int32)
    docs = jnp.sum(jnp.where(hits, documents[None, :], 0), axis=1)

    most = -(-dev_count * min(pair_count, slot_cap) // UNROLL) * UNROLL
    parts = -(-most // LANES)
    near_count = len(near_offsets)
    groups_of = [((index, None),) for index in range(near_count)]
    groups_of += [((near_count + i, 0), (2 * near_count + i, 1)) for i in range(near_count)]
    pay, lists = call(
        functools.partial(
            route_body, rows=rows, size=pass_count, groups_of=groups_of, list_len=list_len
        ),
        [
            shape((dev_count * (rows + TAIL), width), BF16),
            shape((3 * near_count, 3, parts, LANES), jnp.int32),
        ],
        "route",
        in_specs=[smem] + [vmem] * len(pays),
    )(docs, *pays)

    all_queries = dev_count * query_count
    half_rows = all_queries * length // 2
    totals = [
        shape(((2 * all_queries + 1) * length, width), F32),
        shape((2 * all_queries + 1, LANES), F32),
    ]
    sends = [shape((half_rows, width), BF16)] * 2
    def score(blocks, piece, state=()):
        return call(
            functools.partial(
                score_body, piece=piece, count=near_count, begin=not state, length=length
            ),
            totals,
            "score",
            [vmem] * (2 + len(blocks) + len(state)),
            {2 + len(blocks): 0, 3 + len(blocks): 1} if state else {},
            [
                pltpu.SMEM((near_count, 3, parts, LANES), jnp.int32),
                pltpu.SemaphoreType.DMA(()),
            ],
        )(lists, pay, *blocks, *state)

    state = score(near, 0)
    far_raw, *state = lax.optimization_barrier((far_raw, *state))
    far = []
    for index, raw in enumerate(spread(far_raw)):
        last = index == near_count - 1
        acc, sums, *blocks = call(
            functools.partial(far_score_body, piece=near_count + index, length=length),
            totals + [shape(passages.shape, BF16), turned] + (sends if last else []),
            "score_far",
            [vmem] * 5,
            {3: 0, 4: 1},
            [pltpu.SMEM((3, parts, LANES), jnp.int32), pltpu.SemaphoreType.DMA(())],
        )(lists, pay, raw, *state)
        state = (acc, sums)
        far += blocks[:2]
    others, firsts = blocks[2:]

    steps = bits_of(dev_count)[::-1]
    got_others = swap(others, "dev", steps[0])
    got_firsts = swap(firsts, "dev", steps[1])
    def quarters(sums):
        spreads, scores = sums[: 2 * all_queries].reshape(2, 2, 2, all_queries // 4, LANES)
        return [jnp.stack([spreads[half], scores[:, half]]) for half in (0, 1)]

    got_sums = swap(quarters(sums)[1], "dev", steps[0])
    got_sums, *state = lax.optimization_barrier((got_sums, *state))
    acc, sums = score(far, 2 * near_count, state)
    sums = quarters(sums)[0] + got_sums
    levels = len(steps) - 2
    halves = [sums[:, index].reshape((2,) + (2,) * levels + (query_count, LANES)) for index in (0, 1)]
    sums = halves[0]
    for mask in range(1, 2 << levels):
        turned_halves = halves[mask & 1]
        axes = [1 + level for level in range(levels) if mask >> (level + 1) & 1]
        bits = sum(bit for place, bit in enumerate(steps[1:]) if mask >> place & 1)
        sums = sums + swap(jnp.flip(turned_halves, axis=axes), "dev", bits)
    sums = sums.reshape(2, all_queries // 4, LANES)
    quarter = half_rows // 4
    leaving = call(halve_body, [shape((quarter, width), BF16)] * 4, "halve")(
        acc, got_others, got_firsts
    )
    arrived = [swap(rows, "dev", bit) for rows, bit in zip(leaving, steps[1::-1] * 2)]
    send, rest = (
        call(
            functools.partial(merge_body, part=part, length=length),
            shape((quarter, width), kind),
            "merge",
        )(acc, got_others, got_firsts, *arrived[2 * index : 2 * index + 2], sums)
        for index, (part, kind) in enumerate(((1, BF16), (0, F32)))
    )
    for bit in steps[2:-1]:
        rest = rest + swap(send, "dev", bit).astype(F32)
        quarter = quarter // 2
        rest, send = rest[:quarter], rest[quarter:].astype(BF16)
    got = swap(send, "dev", steps[-1])
    grad, loss = call(
        functools.partial(last_body, length=length),
        [shape(queries.shape, F32), shape((1, query_count), F32)],
        "last",
    )(queries, rest, got, sums[:, :query_count])
    return loss.reshape(query_count), grad


def solution(mesh):
    placed = (
        P(("group", "dev"), None, None),
        P(("group", "dev"), None, None),
        P(("group", "dev"), None),
        P(),
    )
    return jax.shard_map(
        local,
        mesh=mesh,
        in_specs=placed,
        out_specs=(P(("group", "dev")), P(("group", "dev"), None, None)),
        check_vma=False,
    )
```

```python
import functools

import jax
import jax.numpy as jnp
from jax import lax
from jax.experimental import pallas as pl
from jax.experimental.pallas import tpu as pltpu
from jax.sharding import PartitionSpec as P

SOFTNESS = 0.02
EPSILON = 1e-06
LANES = 128
TAIL = 16
BASE = 256
UNROLL = 20
SHIFT = 1 << 16
F32 = jnp.float32
BF16 = jnp.bfloat16


def call(body, out_shape, name, in_specs=None, aliases={}, scratch=()):
    kwargs = {} if in_specs is None else {"in_specs": in_specs}
    return pl.pallas_call(
        body,
        out_shape=out_shape,
        input_output_aliases=aliases,
        scratch_shapes=list(scratch),
        name=name,
        cost_estimate=pl.CostEstimate(flops=0, bytes_accessed=0, transcendentals=0),
        compiler_params=pltpu.CompilerParams(vmem_limit_bytes=20 * 1024 * 1024),
        **kwargs,
    )


def unit(values):
    floats = values.astype(F32)
    scale = lax.rsqrt(jnp.sum(floats * floats, axis=-1, keepdims=True) + EPSILON)
    return floats * scale, scale


def pack_body(queries_ref, cand_ref, out_ref):
    count, length, width = queries_ref.shape
    rows = count * length
    out_ref[:rows] = unit(queries_ref[...])[0].astype(BF16).reshape(rows, width)
    ids = jnp.concatenate([cand_ref[index : index + 1] for index in range(count)], axis=1)
    ids = jnp.broadcast_to(ids, (TAIL, LANES))
    high = ids // BASE
    low = ids - high * BASE
    place = lax.broadcasted_iota(jnp.int32, (TAIL, LANES), 0)
    digits = jnp.where(place == 0, high, jnp.where(place == 1, low, 0))
    out_ref[rows:] = digits.astype(F32).astype(BF16)


def turn_units(source, units_ref, turned_ref):
    count = source.shape[0]
    together = min(count, 16)

    def step(index, carry):
        for offset in range(together):
            at = index * together + offset
            units = unit(source[at])[0].astype(BF16)
            units_ref[at] = units
            turned_ref[at] = units.T
        return carry

    lax.fori_loop(0, count // together, step, 0)


def unit_body(*refs):
    half = len(refs) // 3
    for index, source in enumerate(refs[:half]):
        turn_units(source, refs[half + 2 * index], refs[half + 2 * index + 1])


def route_body(docs_ref, *refs, rows, size, groups_of, list_len):
    *pay_refs, out_ref, list_ref = refs
    per_ref = pay_refs[0].shape[0]
    blocks = per_ref * len(pay_refs)
    stride = rows + TAIL
    ids = []
    for index, pay_ref in enumerate(pay_refs):
        for block in range(per_ref):
            start = (index * per_ref + block) * stride
            out_ref[start : start + stride] = pay_ref[block]
            tile = pay_ref[block, rows:].astype(F32)
            ids.append((tile[0:1] * BASE + tile[1:2]).astype(jnp.int32))
    ids = jnp.concatenate(ids, axis=0)
    per_block = LANES // list_len
    queries = blocks * per_block
    block = lax.broadcasted_iota(jnp.int32, (blocks, LANES), 0)
    lane = lax.broadcasted_iota(jnp.int32, (blocks, LANES), 1)
    query = lane // list_len
    source = (block * stride + query * (rows // per_block)).astype(F32)
    quarter = blocks // 4
    region = block // quarter
    moved = block + jnp.where(region == 1, quarter, 0) - jnp.where(region == 2, quarter, 0)
    first = lane % list_len == 0
    target = jnp.where(first, queries + moved * per_block, block * per_block) + query
    target = (target - 2 * queries).astype(F32)
    upper = lax.broadcasted_iota(jnp.int32, (LANES, LANES), 0)
    column = lax.broadcasted_iota(jnp.int32, (LANES, LANES), 1)
    triangle = (upper <= column).astype(F32)
    diagonal = upper == column
    parts = list_ref.shape[2]
    place = lax.broadcasted_iota(jnp.int32, (parts * LANES, LANES), 0).astype(F32)
    leaving = (block >= 2 * quarter) | (first & (region == 1))
    for index, groups in enumerate(groups_of):
        held = jnp.full((blocks, LANES), -1, jnp.int32)
        for place_of in range(size):
            held = jnp.where(ids == docs_ref[index * size + place_of], place_of, held)
        code = held.astype(F32) * SHIFT + source
        for piece, group in groups:
            mask = held >= 0
            if group is not None:
                mask = mask & (leaving if group == 0 else jnp.logical_not(leaving))
            ranks = jnp.dot(mask.astype(F32), triangle, preferred_element_type=F32)
            before = jnp.zeros((1, 1), F32)
            codes = jnp.zeros((parts * LANES, LANES), F32)
            targets = jnp.zeros((parts * LANES, LANES), F32)
            for row_of in range(blocks):
                row = ranks[row_of : row_of + 1]
                slot = jnp.where(mask[row_of : row_of + 1], before + row - 1.0, -1.0)
                here = place == slot
                codes = codes + jnp.where(here, code[row_of : row_of + 1], 0.0)
                targets = targets + jnp.where(here, target[row_of : row_of + 1], 0.0)
                before = before + row[:, LANES - 1 : LANES]
            for kind, found in enumerate((codes, targets + 2.0 * queries / LANES)):
                packed = jnp.sum(found, axis=1, keepdims=True)
                for part in range(parts):
                    value = packed[part * LANES : (part + 1) * LANES]
                    line = jnp.sum(jnp.where(diagonal, value, 0.0), axis=0, keepdims=True)
                    list_ref[piece, kind, part : part + 1] = line.astype(jnp.int32)
            list_ref[piece, 2] = jnp.broadcast_to(before, (parts, LANES)).astype(jnp.int32)


def score_pairs(list_ref, pay_ref, pass_ref, turned_ref, acc_ref, sums_ref, length):
    queries = sums_ref.shape[0] // 2
    count = list_ref[2, 0, 0]

    def step(index, carry):
        pairs = []
        for offset in range(UNROLL):
            slot = index * UNROLL + offset
            part, lane = lax.shift_right_logical(slot, 7), slot & (LANES - 1)
            code = list_ref[0, part, lane]
            row = pl.multiple_of(code & (SHIFT - 1), 16)
            place = lax.shift_right_logical(code, SHIFT.bit_length() - 1)
            pairs.append((list_ref[1, part, lane], pay_ref[pl.ds(row, length)], place))
        logits = [
            jnp.dot(tokens, turned_ref[place], preferred_element_type=F32)
            for _, tokens, place in pairs
        ]
        terms = [jnp.exp(block * (1.0 / SOFTNESS)) for block in logits]
        masses = [jnp.sum(block, axis=1, keepdims=True) for block in terms]
        pulled = [
            jnp.dot(block.astype(BF16), pass_ref[pair[2]], preferred_element_type=F32)
            for block, pair in zip(terms, pairs)
        ]
        done = []
        for (target, _, _), mass, rows in zip(pairs, masses, pulled):
            score = SOFTNESS * jnp.sum(jnp.log(mass), axis=0, keepdims=True)
            exp_score = jnp.exp(score)
            first = target >= queries
            factor = jnp.where(first, 1.0, exp_score)
            done.append((target, rows * (factor / mass), jnp.where(first, score, exp_score)))
        for target, product, value in done:
            at = pl.ds(pl.multiple_of(target * length, length), length)
            acc_ref[at] = acc_ref[at] + product
            sums_ref[pl.ds(target, 1)] = sums_ref[pl.ds(target, 1)] + value
        return carry

    lax.fori_loop(0, lax.div(count + UNROLL - 1, UNROLL), step, 0)


def score_body(lists_ref, pay_ref, *refs, piece, count, begin, length):
    pass_refs, refs = refs[: 2 * count], refs[2 * count :]
    acc_ref, sums_ref, list_ref, sem = refs if begin else refs[2:]
    move = pltpu.make_async_copy(lists_ref.at[piece : piece + count], list_ref, sem)
    move.start()
    if begin:
        acc_ref[...] = jnp.zeros_like(acc_ref)
        sums_ref[...] = jnp.zeros_like(sums_ref)
    move.wait()
    for index in range(count):
        score_pairs(
            list_ref.at[index],
            pay_ref,
            pass_refs[2 * index],
            pass_refs[2 * index + 1],
            acc_ref,
            sums_ref,
            length,
        )


def far_score_body(
    lists_ref, pay_ref, raw_ref, _, __, acc_ref, sums_ref, pass_ref, turned_ref, *refs, piece, length
):
    *send_refs, list_ref, sem = refs
    move = pltpu.make_async_copy(lists_ref.at[piece], list_ref, sem)
    move.start()
    turn_units(raw_ref, pass_ref, turned_ref)
    move.wait()
    score_pairs(list_ref, pay_ref, pass_ref, turned_ref, acc_ref, sums_ref, length)
    if send_refs:
        others_ref, firsts_ref = send_refs
        half = others_ref.shape[0]
        others_ref[...] = acc_ref[half : 2 * half].astype(BF16)
        firsts_ref[...] = acc_ref[3 * half : 4 * half].astype(BF16)


def halve_body(acc_ref, got_others, got_firsts, *send_refs):
    for index, send_ref in enumerate(send_refs):
        got, region = ((got_others, 1), (got_firsts, 5))[index % 2]
        size = send_ref.shape[0]
        at = (1 - index // 2) * size
        own = acc_ref[region * 2 * size + at : region * 2 * size + at + size]
        rest = got[2 * size + at : 2 * size + at + size].astype(F32)
        send_ref[...] = (own + rest).astype(BF16)


def merge_body(acc_ref, others_ref, firsts_ref, got_others, got_firsts, sums_ref, out_ref, *, part, length):
    rows = out_ref.shape[0]
    for index in range(rows // length):
        at = slice(index * length, (index + 1) * length)
        here = slice(part * rows + index * length, part * rows + (index + 1) * length)
        behind = slice(8 * rows + here.start, 8 * rows + here.stop)
        others = acc_ref[here] + others_ref[here].astype(F32) + got_others[at].astype(F32)
        first = acc_ref[behind] + firsts_ref[here].astype(F32) + got_firsts[at].astype(F32)
        query = part * (rows // length) + index
        out_ref[at] = (others - sums_ref[0, query : query + 1] * first).astype(out_ref.dtype)


def query_body(queries_ref, sums_ref, unit_ref, scale_ref, loss_ref):
    count = queries_ref.shape[0]
    losses = []
    for index in range(count):
        score = sums_ref[1, index : index + 1]
        total = sums_ref[0, index : index + 1] + jnp.exp(score)
        losses.append(jnp.log(total) - score)
        units, scale = unit(queries_ref[index])
        unit_ref[index] = units
        scale_ref[index] = scale / total
    losses = jnp.concatenate(losses, axis=0)
    place = lax.broadcasted_iota(jnp.int32, (count, LANES), 0)
    lane = lax.broadcasted_iota(jnp.int32, (count, LANES), 1)
    loss_ref[...] = jnp.sum(jnp.where(place == lane, losses, 0.0), axis=0, keepdims=True)[:, :count]


def last_body(keep_ref, got_ref, unit_ref, scale_ref, grad_ref):
    gradient = (keep_ref[...] + got_ref[...].astype(F32)).reshape(unit_ref.shape)
    units = unit_ref[...]
    along = jnp.sum(units * gradient, axis=-1, keepdims=True)
    grad_ref[...] = (gradient - units * along) * scale_ref[...]


def swap(value, axis, bit):
    size = lax.axis_size(axis)
    return lax.ppermute(value, axis, [(index, index ^ bit) for index in range(size)])


def bits_of(size):
    return [1 << power for power in reversed(range(size.bit_length() - 1))]


def spread_offsets(size):
    offsets = [0]
    for bit in bits_of(size):
        offsets = offsets + [offset ^ bit for offset in offsets]
    return offsets


def spread(block):
    blocks = [block]
    for bit in bits_of(lax.axis_size("group") // 2):
        blocks = blocks + [swap(held, "group", bit) for held in blocks]
    return blocks


def local(queries, passages, candidates, location):
    group_count = lax.axis_size("group")
    dev_count = lax.axis_size("dev")
    device_total = group_count * dev_count
    query_count, length, width = queries.shape
    pass_count, pass_len, _ = passages.shape
    list_len = candidates.shape[1]
    pair_count = query_count * list_len
    rows = query_count * length
    slot_cap = max(2, (3 * pair_count + device_total - 1) // device_total)
    group = lax.axis_index("group")
    dev = lax.axis_index("dev")
    shape = jax.ShapeDtypeStruct

    half_bit = group_count // 2
    far_raw = swap(passages, "group", half_bit)
    near_raw = spread(passages)
    hbm, smem, vmem = (
        pl.BlockSpec(memory_space=space) for space in (pltpu.HBM, pltpu.SMEM, pltpu.VMEM)
    )
    payload = call(
        pack_body,
        shape((rows + TAIL, width), BF16),
        "query_units",
        [vmem, vmem],
    )(queries, candidates)

    *first_bits, low, lowest = bits_of(dev_count)
    pay = payload[None]
    for bit in first_bits:
        pay = jnp.concatenate([pay, swap(pay, "dev", bit)], axis=0)
    turned = shape((pass_count, width, pass_len), BF16)
    near = call(unit_body, [shape(passages.shape, BF16), turned] * len(near_raw), "passage_units")(
        *near_raw
    )
    pay_low = swap(pay, "dev", low)
    pays = [pay, pay_low, swap(pay, "dev", lowest), swap(pay_low, "dev", lowest)]
    pays[3], near = lax.optimization_barrier((pays[3], near))

    near_offsets = spread_offsets(half_bit)
    offsets = near_offsets + [offset ^ half_bit for offset in near_offsets]
    held_rows = jnp.concatenate(
        [
            ((group ^ offset) * dev_count + dev) * pass_count + jnp.arange(pass_count)
            for offset in offsets
        ]
    )
    hits = location[None, :] == held_rows.astype(jnp.int32)[:, None]
    documents = jnp.arange(location.shape[0], dtype=jnp.int32)
    docs = jnp.sum(jnp.where(hits, documents[None, :], 0), axis=1)

    most = -(-dev_count * min(pair_count, slot_cap) // UNROLL) * UNROLL
    parts = -(-most // LANES)
    near_count = len(near_offsets)
    groups_of = [((index, None),) for index in range(near_count)]
    groups_of += [((near_count + i, 0), (2 * near_count + i, 1)) for i in range(near_count)]
    pay, lists = call(
        functools.partial(
            route_body, rows=rows, size=pass_count, groups_of=groups_of, list_len=list_len
        ),
        [
            shape((dev_count * (rows + TAIL), width), BF16),
            shape((3 * near_count, 3, parts, LANES), jnp.int32),
        ],
        "route",
        in_specs=[smem] + [vmem] * len(pays),
    )(docs, *pays)

    all_queries = dev_count * query_count
    half_rows = all_queries * length // 2
    totals = [
        shape(((2 * all_queries + 1) * length, width), F32),
        shape((2 * all_queries + 1, LANES), F32),
    ]
    sends = [shape((half_rows, width), BF16)] * 2
    def score(blocks, piece, state=()):
        return call(
            functools.partial(
                score_body, piece=piece, count=near_count, begin=not state, length=length
            ),
            totals,
            "score",
            [vmem] * (2 + len(blocks) + len(state)),
            {2 + len(blocks): 0, 3 + len(blocks): 1} if state else {},
            [
                pltpu.SMEM((near_count, 3, parts, LANES), jnp.int32),
                pltpu.SemaphoreType.DMA(()),
            ],
        )(lists, pay, *blocks, *state)

    state = score(near, 0)
    far_raw, *state = lax.optimization_barrier((far_raw, *state))
    far = []
    for index, raw in enumerate(spread(far_raw)):
        last = index == near_count - 1
        acc, sums, *blocks = call(
            functools.partial(far_score_body, piece=near_count + index, length=length),
            totals + [shape(passages.shape, BF16), turned] + (sends if last else []),
            "score_far",
            [vmem] * 5,
            {3: 0, 4: 1},
            [pltpu.SMEM((3, parts, LANES), jnp.int32), pltpu.SemaphoreType.DMA(())],
        )(lists, pay, raw, *state)
        state = (acc, sums)
        far += blocks[:2]
    others, firsts = blocks[2:]

    steps = bits_of(dev_count)[::-1]
    got_others = swap(others, "dev", steps[0])
    got_firsts = swap(firsts, "dev", steps[1])
    def quarters(sums):
        spreads, scores = sums[: 2 * all_queries].reshape(2, 2, 2, all_queries // 4, LANES)
        return [jnp.stack([spreads[half], scores[:, half]]) for half in (0, 1)]

    got_sums = swap(quarters(sums)[1], "dev", steps[0])
    got_sums, *state = lax.optimization_barrier((got_sums, *state))
    acc, sums = score(far, 2 * near_count, state)
    sums = quarters(sums)[0] + got_sums
    levels = len(steps) - 2
    halves = [sums[:, index].reshape((2,) + (2,) * levels + (query_count, LANES)) for index in (0, 1)]
    sums = halves[0]
    for mask in range(1, 2 << levels):
        turned_halves = halves[mask & 1]
        axes = [1 + level for level in range(levels) if mask >> (level + 1) & 1]
        bits = sum(bit for place, bit in enumerate(steps[1:]) if mask >> place & 1)
        sums = sums + swap(jnp.flip(turned_halves, axis=axes), "dev", bits)
    sums = sums.reshape(2, all_queries // 4, LANES)
    quarter = half_rows // 4
    leaving = call(halve_body, [shape((quarter, width), BF16)] * 4, "halve")(
        acc, got_others, got_firsts
    )
    arrived = [swap(rows, "dev", bit) for rows, bit in zip(leaving, steps[1::-1] * 2)]
    send, rest = (
        call(
            functools.partial(merge_body, part=part, length=length),
            shape((quarter, width), kind),
            "merge",
        )(acc, got_others, got_firsts, *arrived[2 * index : 2 * index + 2], sums)
        for index, (part, kind) in enumerate(((1, BF16), (0, F32)))
    )
    for bit in steps[2:-1]:
        rest = rest + swap(send, "dev", bit).astype(F32)
        quarter = quarter // 2
        rest, send = rest[:quarter], rest[quarter:].astype(BF16)
    got = swap(send, "dev", steps[-1])
    units, scale, loss = call(
        query_body,
        [shape(queries.shape, F32)] * 2 + [shape((1, query_count), F32)],
        "query_side",
    )(queries, sums[:, :query_count])
    grad = call(last_body, shape(queries.shape, F32), "last")(rest, got, units, scale)
    return loss.reshape(query_count), grad


def solution(mesh):
    placed = (
        P(("group", "dev"), None, None),
        P(("group", "dev"), None, None),
        P(("group", "dev"), None),
        P(),
    )
    return jax.shard_map(
        local,
        mesh=mesh,
        in_specs=placed,
        out_specs=(P(("group", "dev")), P(("group", "dev"), None, None)),
        check_vma=False,
    )
```

```python
import functools

import jax
import jax.numpy as jnp
from jax import lax
from jax.experimental import pallas as pl
from jax.experimental.pallas import tpu as pltpu
from jax.sharding import PartitionSpec as P

SOFTNESS = 0.02
EPSILON = 1e-06
LANES = 128
TAIL = 16
BASE = 256
UNROLL = 20
SHIFT = 1 << 16
F32 = jnp.float32
BF16 = jnp.bfloat16


def call(body, out_shape, name, in_specs=None, aliases={}, scratch=()):
    kwargs = {} if in_specs is None else {"in_specs": in_specs}
    return pl.pallas_call(
        body,
        out_shape=out_shape,
        input_output_aliases=aliases,
        scratch_shapes=list(scratch),
        name=name,
        cost_estimate=pl.CostEstimate(flops=0, bytes_accessed=0, transcendentals=0),
        compiler_params=pltpu.CompilerParams(vmem_limit_bytes=20 * 1024 * 1024),
        **kwargs,
    )


def unit(values):
    floats = values.astype(F32)
    scale = lax.rsqrt(jnp.sum(floats * floats, axis=-1, keepdims=True) + EPSILON)
    return floats * scale, scale


def pack_body(queries_ref, cand_ref, out_ref):
    count, length, width = queries_ref.shape
    rows = count * length
    out_ref[:rows] = unit(queries_ref[...])[0].astype(BF16).reshape(rows, width)
    ids = jnp.concatenate([cand_ref[index : index + 1] for index in range(count)], axis=1)
    ids = jnp.broadcast_to(ids, (TAIL, LANES))
    high = ids // BASE
    low = ids - high * BASE
    place = lax.broadcasted_iota(jnp.int32, (TAIL, LANES), 0)
    digits = jnp.where(place == 0, high, jnp.where(place == 1, low, 0))
    out_ref[rows:] = digits.astype(F32).astype(BF16)


def turn_units(source, units_ref, turned_ref=None):
    count = source.shape[0]
    together = min(count, 16)

    def step(index, carry):
        for offset in range(together):
            at = index * together + offset
            units = unit(source[at])[0].astype(BF16)
            units_ref[at] = units
            if turned_ref is not None:
                turned_ref[at] = units.T
        return carry

    lax.fori_loop(0, count // together, step, 0)


def unit_body(*refs):
    half = len(refs) // 3
    for index, source in enumerate(refs[:half]):
        turn_units(source, refs[half + 2 * index], refs[half + 2 * index + 1])


def route_body(docs_ref, *refs, rows, size, groups_of, list_len):
    *pay_refs, out_ref, list_ref = refs
    per_ref = pay_refs[0].shape[0]
    blocks = per_ref * len(pay_refs)
    stride = rows + TAIL
    ids = []
    for index, pay_ref in enumerate(pay_refs):
        for block in range(per_ref):
            start = (index * per_ref + block) * stride
            out_ref[start : start + stride] = pay_ref[block]
            tile = pay_ref[block, rows:].astype(F32)
            ids.append((tile[0:1] * BASE + tile[1:2]).astype(jnp.int32))
    ids = jnp.concatenate(ids, axis=0)
    per_block = LANES // list_len
    queries = blocks * per_block
    block = lax.broadcasted_iota(jnp.int32, (blocks, LANES), 0)
    lane = lax.broadcasted_iota(jnp.int32, (blocks, LANES), 1)
    query = lane // list_len
    source = (block * stride + query * (rows // per_block)).astype(F32)
    quarter = blocks // 4
    region = block // quarter
    moved = block + jnp.where(region == 1, quarter, 0) - jnp.where(region == 2, quarter, 0)
    first = lane % list_len == 0
    target = jnp.where(first, queries + moved * per_block, block * per_block) + query
    target = (target - 2 * queries).astype(F32)
    upper = lax.broadcasted_iota(jnp.int32, (LANES, LANES), 0)
    column = lax.broadcasted_iota(jnp.int32, (LANES, LANES), 1)
    triangle = (upper <= column).astype(F32)
    diagonal = upper == column
    parts = list_ref.shape[2]
    place = lax.broadcasted_iota(jnp.int32, (parts * LANES, LANES), 0).astype(F32)
    leaving = (block >= 2 * quarter) | (first & (region == 1))
    for index, groups in enumerate(groups_of):
        held = jnp.full((blocks, LANES), -1, jnp.int32)
        for place_of in range(size):
            held = jnp.where(ids == docs_ref[index * size + place_of], place_of, held)
        code = held.astype(F32) * SHIFT + source
        for piece, group in groups:
            mask = held >= 0
            if group is not None:
                mask = mask & (leaving if group == 0 else jnp.logical_not(leaving))
            ranks = jnp.dot(mask.astype(F32), triangle, preferred_element_type=F32)
            before = jnp.zeros((1, 1), F32)
            codes = jnp.zeros((parts * LANES, LANES), F32)
            targets = jnp.zeros((parts * LANES, LANES), F32)
            for row_of in range(blocks):
                row = ranks[row_of : row_of + 1]
                slot = jnp.where(mask[row_of : row_of + 1], before + row - 1.0, -1.0)
                here = place == slot
                codes = codes + jnp.where(here, code[row_of : row_of + 1], 0.0)
                targets = targets + jnp.where(here, target[row_of : row_of + 1], 0.0)
                before = before + row[:, LANES - 1 : LANES]
            for kind, found in enumerate((codes, targets + 2.0 * queries / LANES)):
                packed = jnp.sum(found, axis=1, keepdims=True)
                for part in range(parts):
                    value = packed[part * LANES : (part + 1) * LANES]
                    line = jnp.sum(jnp.where(diagonal, value, 0.0), axis=0, keepdims=True)
                    list_ref[piece, kind, part : part + 1] = line.astype(jnp.int32)
            list_ref[piece, 2] = jnp.broadcast_to(before, (parts, LANES)).astype(jnp.int32)


def score_pairs(list_ref, pay_ref, pass_ref, turned_ref, acc_ref, sums_ref, length):
    queries = sums_ref.shape[0] // 2
    count = list_ref[2, 0, 0]
    contract = (((1,), (1,)), ((), ()))

    def step(index, carry):
        pairs = []
        for offset in range(UNROLL):
            slot = index * UNROLL + offset
            part, lane = lax.shift_right_logical(slot, 7), slot & (LANES - 1)
            code = list_ref[0, part, lane]
            row = pl.multiple_of(code & (SHIFT - 1), 16)
            place = lax.shift_right_logical(code, SHIFT.bit_length() - 1)
            pairs.append((list_ref[1, part, lane], pay_ref[pl.ds(row, length)], place))
        logits = [
            lax.dot_general(tokens, pass_ref[place], contract, preferred_element_type=F32)
            if turned_ref is None
            else jnp.dot(tokens, turned_ref[place], preferred_element_type=F32)
            for _, tokens, place in pairs
        ]
        terms = [jnp.exp(block * (1.0 / SOFTNESS)) for block in logits]
        masses = [jnp.sum(block, axis=1, keepdims=True) for block in terms]
        pulled = [
            jnp.dot(block.astype(BF16), pass_ref[pair[2]], preferred_element_type=F32)
            for block, pair in zip(terms, pairs)
        ]
        done = []
        for (target, _, _), mass, rows in zip(pairs, masses, pulled):
            score = SOFTNESS * jnp.sum(jnp.log(mass), axis=0, keepdims=True)
            exp_score = jnp.exp(score)
            first = target >= queries
            factor = jnp.where(first, 1.0, exp_score)
            done.append((target, rows * (factor / mass), jnp.where(first, score, exp_score)))
        for target, product, value in done:
            at = pl.ds(pl.multiple_of(target * length, length), length)
            acc_ref[at] = acc_ref[at] + product
            sums_ref[pl.ds(target, 1)] = sums_ref[pl.ds(target, 1)] + value
        return carry

    lax.fori_loop(0, lax.div(count + UNROLL - 1, UNROLL), step, 0)


def score_body(lists_ref, pay_ref, *refs, piece, count, begin, length):
    kinds = 2 if begin else 1
    pass_refs, refs = refs[: kinds * count], refs[kinds * count :]
    acc_ref, sums_ref, list_ref, sem = refs if begin else refs[2:]
    move = pltpu.make_async_copy(lists_ref.at[piece : piece + count], list_ref, sem)
    move.start()
    if begin:
        acc_ref[...] = jnp.zeros_like(acc_ref)
        sums_ref[...] = jnp.zeros_like(sums_ref)
    move.wait()
    for index in range(count):
        score_pairs(
            list_ref.at[index],
            pay_ref,
            pass_refs[kinds * index],
            pass_refs[kinds * index + 1] if begin else None,
            acc_ref,
            sums_ref,
            length,
        )


def far_score_body(
    lists_ref, pay_ref, raw_ref, _, __, acc_ref, sums_ref, pass_ref, *refs, piece, length
):
    *send_refs, list_ref, sem = refs
    move = pltpu.make_async_copy(lists_ref.at[piece], list_ref, sem)
    move.start()
    turn_units(raw_ref, pass_ref)
    move.wait()
    score_pairs(list_ref, pay_ref, pass_ref, None, acc_ref, sums_ref, length)
    if send_refs:
        others_ref, firsts_ref = send_refs
        half = others_ref.shape[0]
        others_ref[...] = acc_ref[half : 2 * half].astype(BF16)
        firsts_ref[...] = acc_ref[3 * half : 4 * half].astype(BF16)


def halve_body(acc_ref, got_others, got_firsts, *send_refs):
    for index, send_ref in enumerate(send_refs):
        got, region = ((got_others, 1), (got_firsts, 5))[index % 2]
        size = send_ref.shape[0]
        at = (1 - index // 2) * size
        own = acc_ref[region * 2 * size + at : region * 2 * size + at + size]
        rest = got[2 * size + at : 2 * size + at + size].astype(F32)
        send_ref[...] = (own + rest).astype(BF16)


def merge_body(acc_ref, others_ref, firsts_ref, got_others, got_firsts, sums_ref, out_ref, *, part, length):
    rows = out_ref.shape[0]
    for index in range(rows // length):
        at = slice(index * length, (index + 1) * length)
        here = slice(part * rows + index * length, part * rows + (index + 1) * length)
        behind = slice(8 * rows + here.start, 8 * rows + here.stop)
        others = acc_ref[here] + others_ref[here].astype(F32) + got_others[at].astype(F32)
        first = acc_ref[behind] + firsts_ref[here].astype(F32) + got_firsts[at].astype(F32)
        query = part * (rows // length) + index
        out_ref[at] = (others - sums_ref[0, query : query + 1] * first).astype(out_ref.dtype)


def query_body(queries_ref, sums_ref, unit_ref, scale_ref, loss_ref):
    count = queries_ref.shape[0]
    losses = []
    for index in range(count):
        score = sums_ref[1, index : index + 1]
        total = sums_ref[0, index : index + 1] + jnp.exp(score)
        losses.append(jnp.log(total) - score)
        units, scale = unit(queries_ref[index])
        unit_ref[index] = units
        scale_ref[index] = scale / total
    losses = jnp.concatenate(losses, axis=0)
    place = lax.broadcasted_iota(jnp.int32, (count, LANES), 0)
    lane = lax.broadcasted_iota(jnp.int32, (count, LANES), 1)
    loss_ref[...] = jnp.sum(jnp.where(place == lane, losses, 0.0), axis=0, keepdims=True)[:, :count]


def last_body(keep_ref, got_ref, unit_ref, scale_ref, grad_ref):
    gradient = (keep_ref[...] + got_ref[...].astype(F32)).reshape(unit_ref.shape)
    units = unit_ref[...]
    along = jnp.sum(units * gradient, axis=-1, keepdims=True)
    grad_ref[...] = (gradient - units * along) * scale_ref[...]


def swap(value, axis, bit):
    size = lax.axis_size(axis)
    return lax.ppermute(value, axis, [(index, index ^ bit) for index in range(size)])


def bits_of(size):
    return [1 << power for power in reversed(range(size.bit_length() - 1))]


def spread_offsets(size):
    offsets = [0]
    for bit in bits_of(size):
        offsets = offsets + [offset ^ bit for offset in offsets]
    return offsets


def spread(block):
    blocks = [block]
    for bit in bits_of(lax.axis_size("group") // 2):
        blocks = blocks + [swap(held, "group", bit) for held in blocks]
    return blocks


def local(queries, passages, candidates, location):
    group_count = lax.axis_size("group")
    dev_count = lax.axis_size("dev")
    device_total = group_count * dev_count
    query_count, length, width = queries.shape
    pass_count, pass_len, _ = passages.shape
    list_len = candidates.shape[1]
    pair_count = query_count * list_len
    rows = query_count * length
    slot_cap = max(2, (3 * pair_count + device_total - 1) // device_total)
    group = lax.axis_index("group")
    dev = lax.axis_index("dev")
    shape = jax.ShapeDtypeStruct

    half_bit = group_count // 2
    far_raw = swap(passages, "group", half_bit)
    near_raw = spread(passages)
    hbm, smem, vmem = (
        pl.BlockSpec(memory_space=space) for space in (pltpu.HBM, pltpu.SMEM, pltpu.VMEM)
    )
    payload = call(
        pack_body,
        shape((rows + TAIL, width), BF16),
        "query_units",
        [vmem, vmem],
    )(queries, candidates)

    *first_bits, low, lowest = bits_of(dev_count)
    pay = payload[None]
    for bit in first_bits:
        pay = jnp.concatenate([pay, swap(pay, "dev", bit)], axis=0)
    turned = shape((pass_count, width, pass_len), BF16)
    near = call(unit_body, [shape(passages.shape, BF16), turned] * len(near_raw), "passage_units")(
        *near_raw
    )
    pay_low = swap(pay, "dev", low)
    pays = [pay, pay_low, swap(pay, "dev", lowest), swap(pay_low, "dev", lowest)]
    pays[3], near = lax.optimization_barrier((pays[3], near))

    near_offsets = spread_offsets(half_bit)
    offsets = near_offsets + [offset ^ half_bit for offset in near_offsets]
    held_rows = jnp.concatenate(
        [
            ((group ^ offset) * dev_count + dev) * pass_count + jnp.arange(pass_count)
            for offset in offsets
        ]
    )
    hits = location[None, :] == held_rows.astype(jnp.int32)[:, None]
    documents = jnp.arange(location.shape[0], dtype=jnp.int32)
    docs = jnp.sum(jnp.where(hits, documents[None, :], 0), axis=1)

    most = -(-dev_count * min(pair_count, slot_cap) // UNROLL) * UNROLL
    parts = -(-most // LANES)
    near_count = len(near_offsets)
    groups_of = [((index, None),) for index in range(near_count)]
    groups_of += [((near_count + i, 0), (2 * near_count + i, 1)) for i in range(near_count)]
    pay, lists = call(
        functools.partial(
            route_body, rows=rows, size=pass_count, groups_of=groups_of, list_len=list_len
        ),
        [
            shape((dev_count * (rows + TAIL), width), BF16),
            shape((3 * near_count, 3, parts, LANES), jnp.int32),
        ],
        "route",
        in_specs=[smem] + [vmem] * len(pays),
    )(docs, *pays)

    all_queries = dev_count * query_count
    half_rows = all_queries * length // 2
    totals = [
        shape(((2 * all_queries + 1) * length, width), F32),
        shape((2 * all_queries + 1, LANES), F32),
    ]
    sends = [shape((half_rows, width), BF16)] * 2
    def score(blocks, piece, state=()):
        return call(
            functools.partial(
                score_body, piece=piece, count=near_count, begin=not state, length=length
            ),
            totals,
            "score",
            [vmem] * (2 + len(blocks) + len(state)),
            {2 + len(blocks): 0, 3 + len(blocks): 1} if state else {},
            [
                pltpu.SMEM((near_count, 3, parts, LANES), jnp.int32),
                pltpu.SemaphoreType.DMA(()),
            ],
        )(lists, pay, *blocks, *state)

    state = score(near, 0)
    far_raw, *state = lax.optimization_barrier((far_raw, *state))
    far = []
    for index, raw in enumerate(spread(far_raw)):
        last = index == near_count - 1
        acc, sums, *blocks = call(
            functools.partial(far_score_body, piece=near_count + index, length=length),
            totals + [shape(passages.shape, BF16)] + (sends if last else []),
            "score_far",
            [vmem] * 5,
            {3: 0, 4: 1},
            [pltpu.SMEM((3, parts, LANES), jnp.int32), pltpu.SemaphoreType.DMA(())],
        )(lists, pay, raw, *state)
        state = (acc, sums)
        far += blocks[:1]
    others, firsts = blocks[1:]

    steps = bits_of(dev_count)[::-1]
    got_others = swap(others, "dev", steps[0])
    got_firsts = swap(firsts, "dev", steps[1])
    def quarters(sums):
        spreads, scores = sums[: 2 * all_queries].reshape(2, 2, 2, all_queries // 4, LANES)
        return [jnp.stack([spreads[half], scores[:, half]]) for half in (0, 1)]

    got_sums = swap(quarters(sums)[1], "dev", steps[0])
    got_sums, *state = lax.optimization_barrier((got_sums, *state))
    acc, sums = score(far, 2 * near_count, state)
    sums = quarters(sums)[0] + got_sums
    levels = len(steps) - 2
    halves = [sums[:, index].reshape((2,) + (2,) * levels + (query_count, LANES)) for index in (0, 1)]
    sums = halves[0]
    for mask in range(1, 2 << levels):
        turned_halves = halves[mask & 1]
        axes = [1 + level for level in range(levels) if mask >> (level + 1) & 1]
        bits = sum(bit for place, bit in enumerate(steps[1:]) if mask >> place & 1)
        sums = sums + swap(jnp.flip(turned_halves, axis=axes), "dev", bits)
    sums = sums.reshape(2, all_queries // 4, LANES)
    quarter = half_rows // 4
    leaving = call(halve_body, [shape((quarter, width), BF16)] * 4, "halve")(
        acc, got_others, got_firsts
    )
    arrived = [swap(rows, "dev", bit) for rows, bit in zip(leaving, steps[1::-1] * 2)]
    send, rest = (
        call(
            functools.partial(merge_body, part=part, length=length),
            shape((quarter, width), kind),
            "merge",
        )(acc, got_others, got_firsts, *arrived[2 * index : 2 * index + 2], sums)
        for index, (part, kind) in enumerate(((1, BF16), (0, F32)))
    )
    for bit in steps[2:-1]:
        rest = rest + swap(send, "dev", bit).astype(F32)
        quarter = quarter // 2
        rest, send = rest[:quarter], rest[quarter:].astype(BF16)
    got = swap(send, "dev", steps[-1])
    units, scale, loss = call(
        query_body,
        [shape(queries.shape, F32)] * 2 + [shape((1, query_count), F32)],
        "query_side",
    )(queries, sums[:, :query_count])
    grad = call(last_body, shape(queries.shape, F32), "last")(rest, got, units, scale)
    return loss.reshape(query_count), grad


def solution(mesh):
    placed = (
        P(("group", "dev"), None, None),
        P(("group", "dev"), None, None),
        P(("group", "dev"), None),
        P(),
    )
    return jax.shard_map(
        local,
        mesh=mesh,
        in_specs=placed,
        out_specs=(P(("group", "dev")), P(("group", "dev"), None, None)),
        check_vma=False,
    )
```
